32 devices in a mesh: grp: 8 (over y, x, core), shard: 4 (over z).
Axes of the slice: x: 2, y: 2, z: 4, core: 2. Of those that a mesh axis runs over, the one named last changes fastest.
Arguments:
- left_table: float32 [131072, 400], P(('grp', 'shard')), may hold values from -2.4 to 2.4
- right_table: float32 [131072, 400], P(('grp', 'shard')), may hold values from -2.4 to 2.4
- left_state: float32 [131072], P(('grp', 'shard')), may hold values from 0.1 to 4
- right_state: float32 [131072], P(('grp', 'shard')), may hold values from 0.1 to 4
- relations: float32 [1345, 400], replicated, may hold values from -4.2 to 4.2
- relation_state: float32 [1345], replicated, may hold values from 0.1 to 100000
- source_rows: int32 [288, 1000], P(('grp', 'shard')), may hold values from 0 to 4095
- relation_ids: int32 [288, 1000], P(('grp', 'shard')), may hold values from 0 to 1344
- target_rows: int32 [288, 1000], P(('grp', 'shard')), may hold values from 0 to 4095
- negative_rows: int32 [288, 1000], P(('grp', 'shard')), may hold values from 0 to 4095
- span_sizes: int32 [32, 9], P(('grp', 'shard')), may hold values from 1 to 1000, 6750 in all within a row
Outputs:
- new_left: float32 [131072, 400], P(('grp', 'shard'))
- new_left_state: float32 [131072], P(('grp', 'shard'))
- new_right: float32 [131072, 400], P(('grp', 'shard'))
- new_right_state: float32 [131072], P(('grp', 'shard'))
- new_relations: float32 [1345, 400], replicated
- new_relation_state: float32 [1345], replicated
The draws below stay inside these ranges and needn't reach their ends.
Inputs may be any that keep to these rules, and one draw needn't show every extreme that they name: `source_rows`: local row ids of the device's own source-side rows. `target_rows`: local row ids of the device's own target-side rows. `negative_rows`: negative j of a span names a local row of device j // 250 of the same group; rows may repeat. The first span_sizes edges of a span are live.
All inputs are finite; a program needn't handle non-finite values.
Results may differ from the reference program's by a relative error of at most 0.0017.
Values may be sent and summed in bfloat16 or wider, within the bound.
No kernel may reach another device: no remote copies, remote signals or barrier semaphores. Data moves between devices by JAX's collectives and lax.ppermute only.
A program may use at most 256 MiB of HBM per device.

```python
import math
import jax
import jax.numpy as jnp
import numpy as np
from jax import lax

D = 400
REL = 1345
ROWS_DEV = 4096
SPANS = 9
SPAN = 1000
NEG = 1000
ROUND = 5
NEG_PER = 250
ENT = 131072
NCH = 288
N_GRP = 8
N_SHARD = 4
DEVICES = 32


def set_ends(values, rng, low, top_value):
    longest = values.shape.index(max(values.shape))
    spots = []
    for shift in (0, 1):
        where = [jax.random.randint(jax.random.fold_in(rng, axis), (), 0, length) for axis, length in enumerate(values.shape)]
        where[longest] = (where[longest] + shift) % values.shape[longest]
        spots.append(tuple(where))
    return values.at[spots[0]].set(low).at[spots[1]].set(top_value)


def shard_levels(key, shape, cuts, low, top_value):
    def one(position, shards_of):
        steps = jax.random.uniform(jax.random.fold_in(jax.random.fold_in(key, 6), position), (shards_of,), jnp.float32, low / len(cuts), top_value / len(cuts))
        return jnp.repeat(jnp.exp(steps), shape[position] // shards_of).reshape((-1,) + (1,) * (len(shape) - position - 1))

    gain = one(*cuts[0])
    for cut in cuts[1:]:
        gain = gain * one(*cut)
    return gain


def cumulative_ranks(amount, lean):
    weights = [(1 << 20) // math.isqrt(standing ** lean) + 1 for standing in range(1, amount + 1)]
    spread = 1 + sum(weights) // (1 << 30)
    return np.cumsum(np.array([max(1, weight // spread) for weight in weights]))


def ranked(rng, extent, number_of, slope):
    listing = cumulative_ranks(number_of, slope)
    ticket = jax.random.randint(jax.random.fold_in(rng, 1), extent, 0, int(listing[number_of - 1]))
    rank = jnp.searchsorted(jnp.asarray(listing, jnp.int32), ticket, side="right")
    return jax.random.permutation(jax.random.fold_in(rng, 2), number_of)[rank].astype(jnp.int32)


def split_up(amount, total, most, lean):
    portions = [(1 << 20) // math.isqrt(rank ** lean) + 1 for rank in range(2, amount + 1)]
    rest, holding = total - most - (amount - 1), [1] * (amount - 1)
    while rest > 0:
        free = [i for i in range(amount - 1) if holding[i] < most]
        pool, left = sum([portions[i] for i in free]), rest
        for i in free:
            more = min(most - holding[i], max(1, left * portions[i] // pool), rest)
            holding[i] = holding[i] + more
            rest = rest - more
    return np.array([most] + holding)


def ragged_sizes(rng, amount, total, reach, skew):
    if amount == 2:
        one = jax.random.randint(rng, (), max(1, total - reach), min(reach, total - 1) + 1)
        return jnp.stack([one, total - one])
    sizes = jnp.asarray(split_up(amount, total, reach, skew), jnp.int32)
    twos = (amount - 1) // 2
    giver, receiver = sizes[1:1 + 2 * twos:2], sizes[2:2 + 2 * twos:2]
    slack = jnp.minimum(giver - 1, reach - receiver)
    passed = jax.random.randint(jax.random.fold_in(rng, 1), (twos,), 0, 1 << 20) % (slack + 1)
    sizes = sizes.at[1:1 + 2 * twos:2].set(giver - passed).at[2:2 + 2 * twos:2].set(receiver + passed)
    return sizes[jax.random.permutation(jax.random.fold_in(rng, 2), amount)]


def gaussian(key, dims, spread, bound, shards=(), kind=jnp.bfloat16):
    loudness = shard_levels(key, dims, shards, -0.22, 0.18) if shards else 1.0
    values = jax.random.normal(key, dims, jnp.float32) * spread * loudness
    return jnp.minimum(jnp.maximum(values, -bound), bound).astype(kind)


def setup_inputs(seed: int = 0) -> dict:
    splits = jax.random.split(jax.random.key(seed), 12)
    return {
        "left_table": gaussian(splits[0], (ENT, D), 0.4, 2.4, ((0, 32),), jnp.float32),
        "right_table": gaussian(splits[1], (ENT, D), 0.4, 2.4, ((0, 32),), jnp.float32),
        "left_state": jnp.clip(jnp.exp(math.log(4.0) - 3.6888794 * jax.random.uniform(splits[2], (ENT,), jnp.float32) ** shard_levels(splits[2], (ENT,), ((0, 32),), -0.2, 0.2)), 0.1, 4.0),
        "right_state": jnp.clip(jnp.exp(math.log(4.0) - 3.6888794 * jax.random.uniform(splits[3], (ENT,), jnp.float32) ** shard_levels(splits[3], (ENT,), ((0, 32),), -0.2, 0.2)), 0.1, 4.0),
        "relations": gaussian(splits[4], (REL, D), 0.7, 4.2, (), jnp.float32),
        "relation_state": jnp.clip(jnp.exp(jax.random.uniform(splits[5], (REL,), jnp.float32, math.log(0.1), math.log(100000.0))), 0.1, 100000.0),
        "source_rows": set_ends(jax.random.randint(splits[6], (NCH, SPAN), 0, ROWS_DEV), jax.random.fold_in(splits[6], 1), 0, ROWS_DEV - 1).astype(jnp.int32),
        "relation_ids": set_ends(ranked(splits[7], (NCH, SPAN), REL, 2), jax.random.fold_in(splits[7], 3), 0, REL - 1).astype(jnp.int32),
        "target_rows": set_ends(jax.random.randint(splits[8], (NCH, SPAN), 0, ROWS_DEV), jax.random.fold_in(splits[8], 1), 0, ROWS_DEV - 1).astype(jnp.int32),
        "negative_rows": set_ends(jax.random.randint(splits[9], (NCH, NEG), 0, ROWS_DEV), jax.random.fold_in(splits[9], 1), 0, ROWS_DEV - 1).astype(jnp.int32),
        "span_sizes": jax.vmap(lambda own: ragged_sizes(own, SPANS, SPANS * SPAN * 3 // 4, SPAN, 2))(jax.random.split(splits[10], DEVICES)).reshape((DEVICES, SPANS)).astype(jnp.int32),
    }


LEARN_RATE = 0.1
EPSILON = 1e-08

def complex_mul(left, right):
    middle = left.shape[-1] // 2
    left_real, left_imag = (left[..., :middle], left[..., middle:])
    right_real, right_imag = (right[..., :middle], right[..., middle:])
    return jnp.concatenate([left_real * right_real - left_imag * right_imag, left_real * right_imag + left_imag * right_real], -1)

def conj_mul(grad, other):
    middle = grad.shape[-1] // 2
    grad_real, grad_imag = (grad[..., :middle], grad[..., middle:])
    other_real, other_imag = (other[..., :middle], other[..., middle:])
    return jnp.concatenate([grad_real * other_real + grad_imag * other_imag, grad_imag * other_real - grad_real * other_imag], -1)

def span_terms(source, relation, target, negatives, weights):
    product = complex_mul(source, relation)
    product_b = product.astype(jnp.bfloat16)
    positive = lax.optimization_barrier(jnp.sum(product * target, -1))
    scores = lax.dot_general(product_b, negatives, (((1,), (1,)), ((), ())), preferred_element_type=jnp.float32)
    pos_grad = -jax.nn.sigmoid(-positive) * weights
    neg_grad = (jax.nn.sigmoid(scores) * weights[:, None]).astype(jnp.bfloat16)
    grad_product = pos_grad[:, None] * target + jnp.dot(neg_grad, negatives, preferred_element_type=jnp.float32)
    grad_target = pos_grad[:, None] * product
    grad_negatives = lax.dot_general(neg_grad, product_b, (((0,), (0,)), ((), ())), preferred_element_type=jnp.float32).astype(jnp.bfloat16)
    grad_source = conj_mul(grad_product, relation)
    grad_relation = conj_mul(grad_product, source)
    return (grad_source, grad_relation, grad_target, grad_negatives)

def row_adagrad(table, state, grad):
    new_state = state + lax.optimization_barrier(jnp.mean(grad * grad, -1))
    return (table - LEARN_RATE * grad / (jnp.sqrt(new_state)[:, None] + EPSILON), new_state)

def reference(left_table, right_table, left_state, right_state, relations, relation_state, source_rows, relation_ids, target_rows, negative_rows, span_sizes):
    positions = jnp.arange(SPAN, dtype=jnp.int32)
    owner_block = jnp.arange(NEG, dtype=jnp.int32) // NEG_PER

    def step(carry, index):
        grad_left, grad_right, grad_rel = carry
        device = index // SPANS
        group = device // N_SHARD
        source_ids = device * ROWS_DEV + source_rows[index]
        target_ids = device * ROWS_DEV + target_rows[index]
        negative_ids = (group * N_SHARD + owner_block) * ROWS_DEV + negative_rows[index]
        weights = (positions < span_sizes[device, index % SPANS]).astype(jnp.float32)
        source = left_table[source_ids]
        relation = relations[relation_ids[index]]
        target = right_table[target_ids]
        negatives = right_table[negative_ids].astype(jnp.bfloat16)
        grad_source, grad_relation, grad_target, grad_negatives = span_terms(source, relation, target, negatives, weights)
        grad_left = grad_left.at[source_ids].add(grad_source)
        grad_right = grad_right.at[target_ids].add(grad_target)
        grad_right = grad_right.at[negative_ids].add(grad_negatives.astype(jnp.float32))
        grad_rel = grad_rel.at[relation_ids[index]].add(grad_relation)
        return ((grad_left, grad_right, grad_rel), None)
    start = (jnp.zeros(left_table.shape, jnp.float32), jnp.zeros(right_table.shape, jnp.float32), jnp.zeros(relations.shape, jnp.float32))
    totals, unused = lax.scan(step, start, jnp.arange(source_rows.shape[0], dtype=jnp.int32))
    grad_left, grad_right, grad_rel = totals
    new_left, new_left_state = row_adagrad(left_table, left_state, grad_left)
    new_right, new_right_state = row_adagrad(right_table, right_state, grad_right)
    new_relations, new_relation_state = row_adagrad(relations, relation_state, grad_rel)
    order = jnp.mod(jnp.arange(N_GRP, dtype=jnp.int32) - ROUND, N_GRP)

    def regroup(array):
        blocks = array.reshape((N_GRP, -1) + array.shape[1:])
        return blocks[order].reshape(array.shape)
    return (regroup(new_left), regroup(new_left_state), regroup(new_right), regroup(new_right_state), new_relations, new_relation_state)
```

```python
import functools

import jax
import jax.numpy as jnp
from jax import lax
from jax.experimental import pallas as pl
from jax.experimental.pallas import tpu as pltpu
from jax.sharding import PartitionSpec as P

ROUND = 5
LEARN_RATE = 0.1
EPSILON = 1e-08
LANES = 128
TILE = 256
GROUP = 16
PITCH = 5
CODE = 32767.0
VMEM_LIMIT = 58 * 1024 * 1024
F32 = jnp.float32
BF16 = jnp.bfloat16


def round_up(n, m):
    return -(-n // m) * m


def params(**kw):
    return pltpu.CompilerParams(vmem_limit_bytes=VMEM_LIMIT, **kw)


def cost(flops, nbytes):
    return pl.CostEstimate(flops=int(flops), bytes_accessed=int(nbytes), transcendentals=0)


def whole(shape):
    return pl.BlockSpec(shape, lambda *_: (0,) * len(shape), pipeline_mode=pl.Buffered(1))


def parts_of(width):
    half = width // 2
    rest = half - LANES
    return ((0, LANES), (LANES, rest), (half, LANES), (half + LANES, rest))


def split_kernel(t_ref, o_ref, *, width, cols):
    for b in range(cols // LANES):
        for j, (start, size) in enumerate(parts_of(width)):
            x = t_ref[start : start + size, b * LANES : (b + 1) * LANES]
            if size < LANES:
                x = jnp.concatenate([x, jnp.zeros((LANES - size, LANES), F32)], 0)
            o_ref[pl.ds(4 * LANES * b + j, LANES, stride=4), :] = x.T


def split_rows(table_t, cols):
    width, rows = table_t.shape
    return pl.pallas_call(
        functools.partial(split_kernel, width=width, cols=cols),
        grid=(rows // cols,),
        in_specs=[pl.BlockSpec((width, cols), lambda i: (0, i))],
        out_specs=pl.BlockSpec((4 * cols, LANES), lambda i: (i, 0)),
        out_shape=jax.ShapeDtypeStruct((4 * rows, LANES), F32),
        compiler_params=params(),
        cost_estimate=cost(0, 4 * rows * (width + 512)),
        name="split_rows",
    )(table_t)


def serve_kernel(idx_ref, t_ref, o_ref, tb, *, rows, step):
    @pl.when((pl.program_id(0) == 0) & (pl.program_id(1) == 0))
    def _():
        for k in range(0, rows, step):
            tb[:, k : k + step] = t_ref[:, k : k + step].astype(BF16)

    idx = idx_ref[0, 0].astype(jnp.int16)
    lanes = idx.shape[-1]
    row = lax.broadcasted_iota(jnp.int16, (step, lanes), 0)
    one, zero = jnp.ones((), BF16), jnp.zeros((), BF16)
    acc = jnp.zeros((t_ref.shape[0], lanes), F32)
    for k in range(0, rows, step):
        hot = jnp.where(row == idx - k, one, zero)
        acc += jnp.dot(tb[:, k : k + step], hot, preferred_element_type=F32)
    o_ref[0] = acc.astype(BF16)


def serve(asked, table_t, first, count):
    shards, spans, _, npp = asked.shape
    width, rows = table_t.shape
    return pl.pallas_call(
        functools.partial(serve_kernel, rows=rows, step=512),
        grid=(shards, count),
        in_specs=[
            pl.BlockSpec((1, 1, 1, npp), lambda q, s: (q, s + first, 0, 0)),
            whole((width, rows)),
        ],
        out_specs=pl.BlockSpec((1, width, npp), lambda q, s: (q, 0, s)),
        out_shape=jax.ShapeDtypeStruct((shards, width, count * npp), BF16),
        scratch_shapes=[pltpu.VMEM((width, rows), BF16)],
        compiler_params=params(),
        cost_estimate=cost(2 * width * rows * shards * count * npp, 4 * width * rows),
        name="serve",
    )(asked, table_t)


def four(i):
    return pl.ds(pl.multiple_of(4 * i, 4), 4)


def staged(first, u):
    return pl.ds(PITCH * (first + u), 4)


def column(first, j, size):
    return pl.ds(pl.multiple_of(PITCH * first, 8) + j, size, stride=PITCH)


def add_rows(jobs, span, edge, first, at, n):
    done = []
    for idx, total, stage in jobs:
        ids = [idx[span, edge + u] for u in range(n)]
        grads = [stage[staged(first, at + u), :] for u in range(n)]
        sums = [total[four(i), :] for i in ids]
        for k in range(n):
            new = sums[k] + grads[k]
            for j in range(k):
                new += grads[j] * jnp.where(ids[j] == ids[k], 1.0, 0.0)
            done.append((total, ids[k], new))
    for total, i, new in done:
        total[four(i), :] = new


def tiles_of(count):
    return (count + TILE - 1) // TILE


def edge_kernel(
    src_idx, rel_idx, tgt_idx, live,
    left4, rel4, right4,
    p_ref, pt_ref, src_ref, rel_ref, tgt_ref, gt_ref,
    st_s, st_r, st_t,
):
    span = pl.program_id(0)
    count = live[span]

    def one_tile(tile, _):
        base = pl.multiple_of(tile * TILE, TILE)

        @pl.loop(0, TILE, step=GROUP)
        def _(r0):
            for v in range(0, GROUP, 8):
                first = r0 + v
                ats = [staged(first, u) for u in range(8)]
                for idx, table, stage in (
                    (src_idx, left4, st_s), (rel_idx, rel4, st_r), (tgt_idx, right4, st_t),
                ):
                    rows = [table[four(idx[span, base + first + u]), :] for u in range(8)]
                    for at, row in zip(ats, rows):
                        stage[at, :] = row

        sub = 32
        lane = lax.broadcasted_iota(jnp.int32, (sub, LANES), 1)
        low = lane < 72

        @pl.loop(0, TILE, step=sub)
        def _(r0):
            r0 = pl.multiple_of(r0, sub)
            here = pl.ds(pl.multiple_of(base + r0, sub), sub)
            s, r, t = (
                [st[column(r0, j, sub), :] for j in range(4)]
                for st in (st_s, st_r, st_t)
            )
            re0 = s[0] * r[0] - s[2] * r[2]
            re1 = s[1] * r[1] - s[3] * r[3]
            im0 = s[0] * r[2] + s[2] * r[0]
            im1 = s[1] * r[3] + s[3] * r[1]
            prod = (re0, re1, im0, im1)
            score = jnp.sum(re0 * t[0] + re1 * t[1] + im0 * t[2] + im1 * t[3], -1, keepdims=True)
            row = lax.broadcasted_iota(jnp.int32, (sub, 1), 0) + (base + r0)
            weight = jnp.where(row < count, 1.0, 0.0)
            grad = -(0.5 - 0.5 * jnp.tanh(0.5 * score)) * weight
            for j in range(4):
                src_ref[0, here, j * LANES : (j + 1) * LANES] = s[j]
                rel_ref[0, here, j * LANES : (j + 1) * LANES] = r[j]
                tgt_ref[0, here, j * LANES : (j + 1) * LANES] = grad * t[j]
                gt_ref[column(base + r0, j, sub), :] = grad * prod[j]
            r_a = pltpu.roll(im0, 72, 1)
            r_b = pltpu.roll(im1, 72, 1)
            natural = (
                re0, jnp.where(low, re1, r_a), jnp.where(low, r_a, r_b), jnp.where(low, r_b, 0.0),
            )
            for j in range(4):
                p_ref[0, here, j * LANES : (j + 1) * LANES] = natural[j].astype(BF16)

        width = pt_ref.shape[1]
        here = pl.ds(base, TILE)
        for j in range(4):
            size = min(LANES, width - j * LANES)
            x = p_ref[0, here, j * LANES : (j + 1) * LANES].T
            pt_ref[0, j * LANES : j * LANES + size, here] = x[:size]
        return 0

    lax.fori_loop(0, tiles_of(count), one_tile, 0)


def edges(src_idx, rel_idx, tgt_idx, live, left4, rel4, right4, width):
    spans, length = src_idx.shape
    row_spec = pl.BlockSpec((1, length, 512), lambda s, *_: (s, 0, 0))
    rows_f32 = jax.ShapeDtypeStruct((spans, length, 512), F32)
    return pl.pallas_call(
        edge_kernel,
        grid_spec=pltpu.PrefetchScalarGridSpec(
            num_scalar_prefetch=4,
            grid=(spans,),
            in_specs=[whole(left4.shape), whole(rel4.shape), whole(right4.shape)],
            out_specs=[
                row_spec,
                pl.BlockSpec((1, width, length), lambda s, *_: (s, 0, 0)),
                row_spec,
                row_spec,
                row_spec,
                pl.BlockSpec((PITCH * length, LANES), lambda s, *_: (s, 0)),
            ],
            scratch_shapes=[pltpu.VMEM((PITCH * TILE, LANES), F32)] * 3,
        ),
        out_shape=[
            jax.ShapeDtypeStruct((spans, length, 512), BF16),
            jax.ShapeDtypeStruct((spans, width, length), BF16),
            rows_f32,
            rows_f32,
            rows_f32,
            jax.ShapeDtypeStruct((spans * PITCH * length, LANES), F32),
        ],
        compiler_params=params(),
        cost_estimate=cost(0, 300e6),
        name="edges",
    )(src_idx, rel_idx, tgt_idx, live, left4, rel4, right4)


def target_kernel(tgt_idx, live, gt_ref, gr4):
    span = pl.program_id(0)

    @pl.when(span == 0)
    def _():
        gr4[...] = jnp.zeros(gr4.shape, F32)

    def some(n, _):
        r0 = pl.multiple_of(n * GROUP, GROUP)
        for v in range(0, GROUP, 2):
            add_rows(((tgt_idx, gr4, gt_ref),), span, r0 + v, r0, v, 2)
        return 0

    lax.fori_loop(0, tiles_of(live[span]) * (TILE // GROUP), some, 0)


def target_grads(tgt_idx, live, gt, size):
    spans, length = tgt_idx.shape
    return pl.pallas_call(
        target_kernel,
        grid_spec=pltpu.PrefetchScalarGridSpec(
            num_scalar_prefetch=2,
            grid=(spans,),
            in_specs=[pl.BlockSpec((PITCH * length, LANES), lambda s, *_: (s, 0))],
            out_specs=whole((size, LANES)),
        ),
        out_shape=jax.ShapeDtypeStruct((size, LANES), F32),
        compiler_params=params(),
        cost_estimate=cost(0, 100e6),
        name="target_grads",
    )(tgt_idx, live, gt)


def later_span_kernel(live, neg_ref, p_ref, pt_ref, _, *refs, first):
    span_kernel(live, neg_ref, p_ref, pt_ref, *refs, first=first)


def span_kernel(live, neg_ref, p_ref, pt_ref, gp_ref, gn_ref, negs, acc, *, first):
    shards, width, npp = neg_ref.shape
    count = live[first + pl.program_id(0)]
    for o in range(shards):
        negs[:width, o * npp : (o + 1) * npp] = neg_ref[o]
    negs[width:, :] = jnp.zeros((negs.shape[0] - width, shards * npp), BF16)
    acc[...] = jnp.zeros(acc.shape, F32)

    def step(t, _):
        base = pl.multiple_of(t * TILE, TILE)
        here = pl.ds(base, TILE)
        n = negs[...]
        row = lax.broadcasted_iota(jnp.int32, (TILE, 1), 0) + base
        half = jnp.where(row < count, 0.5, 0.0)
        scores = jnp.dot(p_ref[0, here, :], n, preferred_element_type=F32)
        ng = (half * jnp.tanh(0.5 * scores) + half).astype(BF16)
        gp_ref[0, here, :] = lax.dot_general(ng, n, (((1,), (1,)), ((), ())), preferred_element_type=F32)
        acc[...] += jnp.dot(pt_ref[0, :, here], ng, preferred_element_type=F32)
        return 0

    lax.fori_loop(0, tiles_of(count), step, 0)
    for o in range(shards):
        gn_ref[o] = acc[:, o * npp : (o + 1) * npp].astype(BF16)


def span_grads(live, negatives, p, pt, grad_products, first, count):
    shards, width, lanes = negatives.shape
    npp = lanes // count
    spans, length, _ = p.shape
    later = grad_products is not None
    return pl.pallas_call(
        functools.partial(later_span_kernel if later else span_kernel, first=first),
        grid_spec=pltpu.PrefetchScalarGridSpec(
            num_scalar_prefetch=1,
            grid=(count,),
            in_specs=[
                pl.BlockSpec((shards, width, npp), lambda s, *_: (0, 0, s)),
                pl.BlockSpec((1, length, 512), lambda s, *_: (s + first, 0, 0)),
                pl.BlockSpec((1, width, length), lambda s, *_: (s + first, 0, 0)),
            ]
            + ([pl.BlockSpec(memory_space=pl.ANY)] if later else []),
            out_specs=[
                pl.BlockSpec((1, length, 512), lambda s, *_: (s + first, 0, 0)),
                pl.BlockSpec((shards, width, npp), lambda s, *_: (0, 0, s)),
            ],
            scratch_shapes=[
                pltpu.VMEM((512, shards * npp), BF16),
                pltpu.VMEM((width, shards * npp), F32),
            ],
        ),
        out_shape=[
            jax.ShapeDtypeStruct((spans, length, 512), F32),
            jax.ShapeDtypeStruct((shards, width, lanes), BF16),
        ],
        input_output_aliases={4: 0} if later else {},
        compiler_params=params(),
        cost_estimate=cost(count * 6 * length * 512 * shards * npp, 8 * count * length * 512),
        name="span_grads",
    )(live, negatives, p, pt, *([grad_products] if later else []))


def source_kernel(
    src_idx, rel_idx, live, gp_ref, src_ref, rel_ref, tgt_ref, gl_in, gk_in, gl4, gk4, st_s, st_r, *, first
):
    span = pl.program_id(0)

    @pl.when(span == 0)
    def _():
        if gl_in is None:
            gl4[...] = jnp.zeros(gl4.shape, F32)
            gk4[...] = jnp.zeros(gk4.shape, F32)
        else:
            gl4[...] = gl_in[...]
            gk4[...] = gk_in[...]

    def one_tile(tile, _):
        base = pl.multiple_of(tile * TILE, TILE)
        sub = 32
        lane = lax.broadcasted_iota(jnp.int32, (sub, LANES), 1)
        low = lane < 72

        @pl.loop(0, TILE, step=sub)
        def _(r0):
            r0 = pl.multiple_of(r0, sub)
            here = pl.ds(pl.multiple_of(base + r0, sub), sub)
            n, s, r, t = (
                [ref[0, here, j * LANES : (j + 1) * LANES] for j in range(4)]
                for ref in (gp_ref, src_ref, rel_ref, tgt_ref)
            )
            re0 = n[0] + t[0]
            re1 = n[1] + t[1]
            im0 = pltpu.roll(jnp.where(low, n[2], n[1]), 56, 1) + t[2]
            im1 = pltpu.roll(jnp.where(low, n[3], n[2]), 56, 1) + t[3]
            for other, stage in ((r, st_s), (s, st_r)):
                grads = (
                    re0 * other[0] + im0 * other[2],
                    re1 * other[1] + im1 * other[3],
                    im0 * other[0] - re0 * other[2],
                    im1 * other[1] - re1 * other[3],
                )
                for j in range(4):
                    stage[column(r0, j, sub), :] = grads[j]

        @pl.loop(0, TILE, step=GROUP)
        def _(r0):
            for v in range(0, GROUP, 2):
                add_rows(((src_idx, gl4, st_s), (rel_idx, gk4, st_r)), first + span, base + r0 + v, r0, v, 2)

        return 0

    lax.fori_loop(0, tiles_of(live[first + span]), one_tile, 0)


def first_source_kernel(src_idx, rel_idx, live, gp, src, rel, tgt, gl4, gk4, st_s, st_r, *, first):
    source_kernel(src_idx, rel_idx, live, gp, src, rel, tgt, None, None, gl4, gk4, st_s, st_r, first=first)


def source_grads(src_idx, rel_idx, live, gp, src, rel, tgt, totals, sizes, first, count):
    spans, length = src_idx.shape
    row_spec = pl.BlockSpec((1, length, 512), lambda s, *_: (s + first, 0, 0))
    outs = [whole((n, LANES)) for n in sizes]
    body = first_source_kernel if totals is None else source_kernel
    return pl.pallas_call(
        functools.partial(body, first=first),
        grid_spec=pltpu.PrefetchScalarGridSpec(
            num_scalar_prefetch=3,
            grid=(count,),
            in_specs=[row_spec] * 4 + ([] if totals is None else outs),
            out_specs=outs,
            scratch_shapes=[pltpu.VMEM((PITCH * TILE, LANES), F32)] * 2,
        ),
        out_shape=[jax.ShapeDtypeStruct((n, LANES), F32) for n in sizes],
        compiler_params=params(),
        cost_estimate=cost(0, 30e6 * count),
        name="source_grads",
    )(src_idx, rel_idx, live, gp, src, rel, tgt, *(totals or ()))


def joined(ref, b, width):
    return [
        ref[pl.ds(4 * LANES * b + j, LANES, stride=4), :].T[:size]
        for j, (_, size) in enumerate(parts_of(width))
    ]


def rotate_kernel(me, x_ref, o_ref):
    o_ref[...] = x_ref[...]


def rotated(x, me, n):
    block = (x.shape[0] // n, x.shape[1])
    return pl.pallas_call(
        rotate_kernel,
        grid_spec=pltpu.PrefetchScalarGridSpec(
            num_scalar_prefetch=1,
            grid=(n,),
            in_specs=[pl.BlockSpec(block, lambda k, me: (lax.rem(k + me[0], n), 0))],
            out_specs=pl.BlockSpec(block, lambda k, me: (k, 0)),
        ),
        out_shape=jax.ShapeDtypeStruct(x.shape, F32),
        compiler_params=params(),
        cost_estimate=cost(0, 8 * x.size),
        name="rotated",
    )(me.reshape(1).astype(jnp.int32), x)


def summed_blocks(x, axis, held):
    n = lax.axis_size(axis)
    rows = x.shape[0] // n
    total = after(x[:rows], held)
    for k in range(1, n):
        total += lax.ppermute(x[k * rows : (k + 1) * rows], axis, [(i, (i + k) % n) for i in range(n)])
    return total


def relation_kernel(g_ref, t_ref, s_ref, _, o_ref, *, width, rows, spare):
    grads = [g_ref[pl.ds(j, rows, stride=4), :] for j in range(4)]
    square = grads[0] * grads[0] + grads[1] * grads[1] + grads[2] * grads[2] + grads[3] * grads[3]
    state = s_ref[...] + jnp.sum(square, -1, keepdims=True) * (1.0 / width)
    scale = LEARN_RATE / (jnp.sqrt(state) + EPSILON)
    lane = lax.broadcasted_iota(jnp.int32, (rows, LANES), 1)
    for j in range(4):
        new = t_ref[pl.ds(j, rows, stride=4), :] - grads[j] * scale
        if j == 1:
            new = jnp.where(lane == spare, state, new)
        o_ref[pl.ds(j, rows, stride=4), :] = new


def update_relations(g4, t4, state, held, width):
    rows = state.shape[0]
    spare = parts_of(width)[1][1]
    full = [pl.BlockSpec(x.shape, lambda: (0, 0)) for x in (g4, t4, state)]
    return pl.pallas_call(
        functools.partial(relation_kernel, width=width, rows=rows, spare=spare),
        in_specs=full + [pl.BlockSpec(memory_space=pl.ANY)],
        out_specs=full[0],
        out_shape=jax.ShapeDtypeStruct(g4.shape, F32),
        compiler_params=params(),
        cost_estimate=cost(0, 3e6),
        name="update_relations",
    )(g4, t4, state, held)


def join_kernel(g_ref, o_ref, s_ref, *, width, cols):
    spare = parts_of(width)[1][1]
    for b in range(cols // LANES):
        here = slice(b * LANES, min((b + 1) * LANES, o_ref.shape[1]))
        count = here.stop - here.start
        for j, (start, size) in enumerate(parts_of(width)):
            x = g_ref[pl.ds(4 * LANES * b + j, LANES, stride=4), :].T
            o_ref[start : start + size, here] = x[:size, :count]
            if j == 1:
                s_ref[:, here] = x[spare : spare + 1, :count]


def join_relations(rows4, width, kinds):
    return pl.pallas_call(
        functools.partial(join_kernel, width=width, cols=rows4.shape[0] // 4),
        in_specs=[pl.BlockSpec(rows4.shape, lambda: (0, 0))],
        out_specs=[pl.BlockSpec((width, kinds), lambda: (0, 0)), pl.BlockSpec((1, kinds), lambda: (0, 0))],
        out_shape=[jax.ShapeDtypeStruct((width, kinds), F32), jax.ShapeDtypeStruct((1, kinds), F32)],
        compiler_params=params(),
        cost_estimate=cost(0, 4 * kinds * (width + 512)),
        name="join_relations",
    )(rows4)


def update(grad, t_ref, s_ref, q_ref, m_ref, start, size):
    here = slice(start, start + size)
    width = t_ref.shape[0]
    state = s_ref[0:1, here] + jnp.sum(grad * grad, 0, keepdims=True) * (1.0 / width)
    new = t_ref[:, here] - grad * (LEARN_RATE / (jnp.sqrt(state) + EPSILON))
    top = jnp.max(jnp.abs(new), 0, keepdims=True)
    code = new * (CODE / jnp.maximum(top, 1e-30))
    q_ref[:, here] = jnp.round(code).astype(jnp.int32).astype(jnp.int16)
    m_ref[0:1, here] = top
    m_ref[1:2, here] = state


def left_kernel(g_ref, t_ref, s_ref, q_ref, m_ref, *, width, cols):
    for b in range(cols // LANES):
        grad = jnp.concatenate(joined(g_ref, b, width), 0)
        update(grad, t_ref, s_ref, q_ref, m_ref, b * LANES, LANES)


def coded_shapes(width, rows):
    return [jax.ShapeDtypeStruct((width, rows), jnp.int16), jax.ShapeDtypeStruct((2, rows), F32)]


def update_left(g4, table_t, state, cols, start, blocks):
    width, rows = table_t.shape
    return pl.pallas_call(
        functools.partial(left_kernel, width=width, cols=cols),
        grid=(blocks,),
        in_specs=[
            pl.BlockSpec((4 * cols, LANES), lambda i: (i + start, 0)),
            pl.BlockSpec((width, cols), lambda i: (0, i + start)),
            pl.BlockSpec((1, cols), lambda i: (0, i + start)),
        ],
        out_specs=[pl.BlockSpec((width, cols), lambda i: (0, i)), pl.BlockSpec((2, cols), lambda i: (0, i))],
        out_shape=coded_shapes(width, blocks * cols),
        compiler_params=params(),
        cost_estimate=cost(0, 10 * blocks * cols * width),
        name="update_left",
    )(g4, table_t, state)


def negative_sum(acc, idx_ref, b_ref, cols, step, start=0):
    shards, _, lanes = b_ref.shape
    row = lax.broadcasted_iota(jnp.int16, (cols, step), 0)
    one, zero = jnp.ones((), BF16), jnp.zeros((), BF16)
    for q in range(shards):
        for k in range(0, lanes, step):
            idx = (idx_ref[q, :, k : k + step] - (pl.program_id(0) + start) * cols).astype(jnp.int16)
            hot = jnp.where(row == idx, one, zero)
            acc += lax.dot_general(
                b_ref[q, :, k : k + step], hot, (((1,), (1,)), ((), ())), preferred_element_type=F32
            )
    return acc


def first_spread_kernel(idx_ref, b_ref, o_ref, *, cols, step):
    o_ref[...] = negative_sum(jnp.zeros(o_ref.shape, F32), idx_ref, b_ref, cols, step)


def spread_kernel(g_ref, g4_ref, idx_ref, b_ref, o_ref, *, cols, step):
    o_ref[...] = negative_sum(g_ref[...], idx_ref, b_ref, cols, step)
    width = o_ref.shape[0]
    for b in range(cols // LANES):
        for (start, size), x in zip(parts_of(width), joined(g4_ref, b, width)):
            o_ref[start : start + size, b * LANES : (b + 1) * LANES] += x


def spread_update_kernel(g_ref, idx_ref, b_ref, t_ref, s_ref, q_ref, m_ref, acc, *, cols, step, start):
    acc[...] = negative_sum(g_ref[...], idx_ref, b_ref, cols, step, start)
    for b in range(cols // LANES):
        update(acc[:, b * LANES : (b + 1) * LANES], t_ref, s_ref, q_ref, m_ref, b * LANES, LANES)


def spread(grads, idx, returned, rows, cols):
    shards, width, lanes = returned.shape
    block = pl.BlockSpec((width, cols), lambda i: (0, i))
    return pl.pallas_call(
        functools.partial(
            spread_kernel if grads else first_spread_kernel,
            cols=cols, step=2 * LANES if lanes % 256 == 0 else LANES,
        ),
        grid=(rows // cols,),
        in_specs=([block, pl.BlockSpec((4 * cols, LANES), lambda i: (i, 0))] if grads else [])
        + [whole(idx.shape), whole(returned.shape)],
        out_specs=block,
        out_shape=jax.ShapeDtypeStruct((width, rows), F32),
        compiler_params=params(),
        cost_estimate=cost(2 * width * rows * shards * lanes, 8 * width * rows),
        name="spread",
    )(*grads, idx, returned)


def spread_update(grad_t, idx, returned, table_t, state, cols, start, blocks):
    width, rows = grad_t.shape
    shards, _, lanes = returned.shape
    here = pl.BlockSpec((width, cols), lambda i: (0, i + start))
    return pl.pallas_call(
        functools.partial(
            spread_update_kernel, cols=cols, step=2 * LANES if lanes % 256 == 0 else LANES, start=start
        ),
        grid=(blocks,),
        in_specs=[
            here, whole(idx.shape), whole(returned.shape), here, pl.BlockSpec((1, cols), lambda i: (0, i + start)),
        ],
        out_specs=[pl.BlockSpec((width, cols), lambda i: (0, i)), pl.BlockSpec((2, cols), lambda i: (0, i))],
        out_shape=coded_shapes(width, blocks * cols),
        scratch_shapes=[pltpu.VMEM((width, cols), F32)],
        compiler_params=params(),
        cost_estimate=cost(2 * width * blocks * cols * shards * lanes, 8 * width * blocks * cols),
        name="spread_update",
    )(grad_t, idx, returned, table_t, state)


def decode_kernel(m_ref, *refs, ways):
    code = sum(ref[...].astype(jnp.int32) for ref in refs[:ways])
    refs[-1][...] = code.astype(F32) * (m_ref[0:1, :] * (1.0 / CODE))


def decode(codes, meta, rows, cols, start, table_t):
    width, count = codes[0].shape
    ways = len(codes)
    block = pl.BlockSpec((width, cols), lambda i: (0, i))
    return pl.pallas_call(
        functools.partial(decode_kernel, ways=ways),
        grid=(count // cols,),
        in_specs=[pl.BlockSpec((2, cols), lambda i: (0, i))]
        + [block] * ways
        + ([] if table_t is None else [pl.BlockSpec(memory_space=pl.ANY)]),
        out_specs=pl.BlockSpec((width, cols), lambda i: (0, i + start)),
        out_shape=jax.ShapeDtypeStruct((width, rows), F32),
        input_output_aliases={} if table_t is None else {1 + ways: 0},
        compiler_params=params(),
        cost_estimate=cost(0, 6 * width * count),
        name="decode",
    )(meta, *codes, *([] if table_t is None else [table_t]))


def passed_along(block, axis, distance):
    devices = range(lax.axis_size(axis))
    route = [((i - distance) % len(devices), i) for i in devices]
    return lax.ppermute(block, axis, route)


def corner_senders(n):
    return [i for i in range(n) if i % 4 == 1]


def handed_over(halves, held):
    (first, meta_a), (second, meta_b) = halves
    n = lax.axis_size("grp")
    turning = corner_senders(n)
    there = lax.ppermute(first, "grp", [(i, (i + ROUND - 1) % n) for i in turning])
    straight = lax.ppermute(first, "grp", [(i, (i + ROUND) % n) for i in range(n) if i not in turning])
    other = passed_along(second, "grp", ROUND)
    metas = [passed_along(m, "grp", ROUND) for m in (meta_a, meta_b)]
    here = lax.ppermute(
        after(there, *held), "grp", [((i + ROUND - 1) % n, (i + ROUND) % n) for i in turning]
    )
    return ((straight, here), metas[0]), ((other,), metas[1])


def decoded(arrived, rows, cols, held):
    table, start = None, 0
    for codes, meta in arrived:
        table = decode((after(codes[0], *held), *codes[1:]), meta, rows, cols, start, table)
        start += codes[0].shape[1] // cols
    return table, jnp.concatenate([meta[1] for _, meta in arrived])


def exchanged(blocks):
    return lax.all_to_all(blocks, "shard", split_axis=0, concat_axis=0, tiled=True)


def after(value, *others):
    return lax.optimization_barrier((value, *others))[0]


def local(
    left_table,
    right_table,
    left_state,
    right_state,
    relations,
    relation_state,
    source_rows,
    relation_ids,
    target_rows,
    negative_rows,
    span_sizes,
):
    shards = lax.axis_size("shard")
    spans, span_len = source_rows.shape
    neg_per = negative_rows.shape[1] // shards
    npp = round_up(neg_per, LANES)
    rows, width = left_table.shape
    kinds = relations.shape[0]
    kinds_up = round_up(kinds, LANES)
    length = round_up(span_len, TILE)

    left_t, right_t, rel_t = left_table.T, right_table.T, relations.T
    live = span_sizes[0]

    ids = negative_rows.reshape(spans, shards, neg_per)
    ids = jnp.pad(ids, ((0, 0), (0, 0), (0, npp - neg_per)), constant_values=-1)
    asked = lax.all_to_all(ids.transpose(1, 0, 2), "shard", split_axis=0, concat_axis=0, tiled=True)
    asked_lanes = asked.reshape(shards, spans, 1, npp)

    src_idx, rel_idx, tgt_idx = (
        jnp.pad(a, ((0, 0), (0, length - span_len))) for a in (source_rows, relation_ids, target_rows)
    )
    rel_t_up = jnp.pad(rel_t, ((0, 0), (0, kinds_up - kinds)))

    third = -(-spans // 3)
    (c0, c1, c2) = [(a, min(third, spans - a)) for a in range(0, spans, third)]

    served0 = serve(asked_lanes, right_t, *c0)
    fetched0 = exchanged(served0)
    served1 = serve(after(asked_lanes, served0), right_t, *c1)
    served2 = serve(after(asked_lanes, served1), right_t, *c2)
    left4 = split_rows(after(left_t, served2), 512)
    right4 = split_rows(after(right_t, served2), 512)
    rel4 = split_rows(after(rel_t_up, served2), kinds_up)

    fetched1 = exchanged(after(served1, left4, right4, rel4))
    p, pt, src, rel, tgt, gt = edges(
        src_idx, rel_idx, tgt_idx, live, after(left4, fetched0), rel4, right4, width
    )

    fetched2 = exchanged(after(served2, p))
    gp, gn0 = span_grads(live, after(fetched0, fetched1), p, pt, None, *c0)
    gp, gn1 = span_grads(live, fetched1, p, pt, gp, *c1)
    sizes = (4 * rows, 4 * kinds_up)
    sums = functools.partial(source_grads, src_idx, rel_idx, live)
    totals = sums(gp, src, rel, tgt, None, sizes, *c0)

    returned0 = exchanged(after(gn0, totals[1], fetched2))
    gp, gn2 = span_grads(live, fetched2, p, pt, after(gp, totals[1]), *c2)
    gl4, gk4 = sums(gp, src, rel, tgt, totals, sizes, c1[0], c1[1] + c2[1])

    returned1 = exchanged(after(gn1, gk4, returned0))
    rel_rotated = rotated(gk4, lax.axis_index("grp"), lax.axis_size("grp"))
    lanes0, lanes1, lanes2 = (
        asked[:, a : a + n].reshape(shards, 1, n * npp) for a, n in (c0, c1, c2)
    )
    grad_right = spread((), lanes0, after(returned0, rel_rotated), rows, 512)
    blocks = rows // 512
    halves = ((0, blocks // 2), (blocks // 2, blocks - blocks // 2))
    left_in = after(left_t, grad_right)
    coded_left = [tuple(update_left(gl4, left_in, left_state[None], 512, *half)) for half in halves]
    rel_total4 = summed_blocks(rel_rotated, "grp", coded_left[1][1])
    rel_sum4 = lax.psum(rel_total4, "shard")

    returned2 = exchanged(after(gn2, rel_total4, returned1))
    gr4 = target_grads(tgt_idx, live, after(gt, rel_total4, returned1), 4 * rows)
    moved_left = handed_over(coded_left, (gr4,))
    grad_right = spread((grad_right, gr4), lanes1, returned1, rows, 512)
    grad_right = after(grad_right, *moved_left[0][0], *moved_left[1][0])

    coded = []
    for half in halves:
        coded.append(
            tuple(spread_update(grad_right, lanes2, returned2, right_t, right_state[None], 512, *half))
        )
        grad_right = after(grad_right, coded[-1][1])
    new_left, new_left_state = decoded(moved_left, rows, 512, (coded[1][1],))
    moved_right = handed_over(coded, (coded[1][1],))
    new_right, new_right_state = decoded(moved_right, rows, 512, (new_left,))
    slice_rows = kinds_up // lax.axis_size("grp")
    place = lax.axis_index("grp") * slice_rows
    own_rel4 = lax.dynamic_slice(rel4, (4 * place, 0), (4 * slice_rows, LANES))
    own_state = lax.dynamic_slice(
        jnp.pad(relation_state, (0, kinds_up - kinds))[:, None], (place, 0), (slice_rows, 1)
    )
    new_rel4 = update_relations(rel_sum4, own_rel4, own_state, coded[0][1], width)
    new_rel4 = lax.all_gather(new_rel4, "grp", axis=0, tiled=True)
    new_rel_t, new_relation_state = join_relations(new_rel4, width, kinds)
    return (new_left.T, new_left_state, new_right.T, new_right_state, new_rel_t.T, new_relation_state[0])


def solution(mesh):
    rows2, rows1 = P(("grp", "shard"), None), P(("grp", "shard"))
    return jax.shard_map(
        local,
        mesh=mesh,
        in_specs=(rows2, rows2, rows1, rows1, P(), P(), rows2, rows2, rows2, rows2, rows2),
        out_specs=(rows2, rows1, rows2, rows1, P(), P()),
        check_vma=False,
    )
```

```python
import functools

import jax
import jax.numpy as jnp
from jax import lax
from jax.experimental import pallas as pl
from jax.experimental.pallas import tpu as pltpu
from jax.sharding import PartitionSpec as P

ROUND = 5
LEARN_RATE = 0.1
EPSILON = 1e-08
LANES = 128
TILE = 256
GROUP = 16
PITCH = 5
CODE = 32767.0
VMEM_LIMIT = 58 * 1024 * 1024
F32 = jnp.float32
BF16 = jnp.bfloat16


def round_up(n, m):
    return -(-n // m) * m


def params(**kw):
    return pltpu.CompilerParams(vmem_limit_bytes=VMEM_LIMIT, **kw)


def cost(flops, nbytes):
    return pl.CostEstimate(flops=int(flops), bytes_accessed=int(nbytes), transcendentals=0)


def whole(shape):
    return pl.BlockSpec(shape, lambda *_: (0,) * len(shape), pipeline_mode=pl.Buffered(1))


def parts_of(width):
    half = width // 2
    rest = half - LANES
    return ((0, LANES), (LANES, rest), (half, LANES), (half + LANES, rest))


def split_kernel(t_ref, o_ref, *, width, cols):
    for b in range(cols // LANES):
        for j, (start, size) in enumerate(parts_of(width)):
            x = t_ref[start : start + size, b * LANES : (b + 1) * LANES]
            if size < LANES:
                x = jnp.concatenate([x, jnp.zeros((LANES - size, LANES), F32)], 0)
            o_ref[pl.ds(4 * LANES * b + j, LANES, stride=4), :] = x.T


def split_rows(table_t, cols):
    width, rows = table_t.shape
    rows = round_up(rows, cols)
    return pl.pallas_call(
        functools.partial(split_kernel, width=width, cols=cols),
        grid=(rows // cols,),
        in_specs=[pl.BlockSpec((width, cols), lambda i: (0, i))],
        out_specs=pl.BlockSpec((4 * cols, LANES), lambda i: (i, 0)),
        out_shape=jax.ShapeDtypeStruct((4 * rows, LANES), F32),
        compiler_params=params(),
        cost_estimate=cost(0, 4 * rows * (width + 512)),
        name="split_rows",
    )(table_t)


def serve_kernel(idx_ref, t_ref, o_ref, tb, *, rows, step):
    @pl.when((pl.program_id(0) == 0) & (pl.program_id(1) == 0))
    def _():
        for k in range(0, rows, step):
            tb[:, k : k + step] = t_ref[:, k : k + step].astype(BF16)

    idx = idx_ref[0, 0].astype(jnp.int16)
    lanes = idx.shape[-1]
    row = lax.broadcasted_iota(jnp.int16, (step, lanes), 0)
    one, zero = jnp.ones((), BF16), jnp.zeros((), BF16)
    acc = jnp.zeros((t_ref.shape[0], lanes), F32)
    for k in range(0, rows, step):
        hot = jnp.where(row == idx - k, one, zero)
        acc += jnp.dot(tb[:, k : k + step], hot, preferred_element_type=F32)
    o_ref[0] = acc.astype(BF16)


def serve(asked, table_t, first, count):
    shards, spans, _, npp = asked.shape
    width, rows = table_t.shape
    return pl.pallas_call(
        functools.partial(serve_kernel, rows=rows, step=512),
        grid=(shards, count),
        in_specs=[
            pl.BlockSpec((1, 1, 1, npp), lambda q, s: (q, s + first, 0, 0)),
            whole((width, rows)),
        ],
        out_specs=pl.BlockSpec((1, width, npp), lambda q, s: (q, 0, s)),
        out_shape=jax.ShapeDtypeStruct((shards, width, count * npp), BF16),
        scratch_shapes=[pltpu.VMEM((width, rows), BF16)],
        compiler_params=params(),
        cost_estimate=cost(2 * width * rows * shards * count * npp, 4 * width * rows),
        name="serve",
    )(asked, table_t)


def four(i):
    return pl.ds(pl.multiple_of(4 * i, 4), 4)


def staged(first, u):
    return pl.ds(pl.multiple_of(PITCH * first, 8) + PITCH * u, 4)


def column(first, j, size):
    return pl.ds(pl.multiple_of(PITCH * first, 8) + j, size, stride=PITCH)


def add_rows(jobs, span, edge, first, at, n):
    done = []
    for idx, total, stage in jobs:
        ids = [idx[span, edge + u] for u in range(n)]
        grads = [stage[staged(first, at + u), :] for u in range(n)]
        sums = [total[four(i), :] for i in ids]
        for k in range(n):
            new = sums[k] + grads[k]
            for j in range(k):
                new += grads[j] * jnp.where(ids[j] == ids[k], 1.0, 0.0)
            done.append((total, ids[k], new))
    for total, i, new in done:
        total[four(i), :] = new


def tiles_of(count):
    return (count + TILE - 1) // TILE


def edge_kernel(
    src_idx, rel_idx, tgt_idx, live,
    left4, rel4, right4,
    p_ref, pt_ref, src_ref, rel_ref, tgt_ref, gt_ref,
    st_s, st_r, st_t,
):
    span = pl.program_id(0)
    count = live[span]

    def one_tile(tile, _):
        base = pl.multiple_of(tile * TILE, TILE)

        @pl.loop(0, TILE, step=GROUP)
        def _(r0):
            for v in range(0, GROUP, 8):
                first = r0 + v
                ats = [staged(first, u) for u in range(8)]
                for idx, table, stage in (
                    (src_idx, left4, st_s), (rel_idx, rel4, st_r), (tgt_idx, right4, st_t),
                ):
                    rows = [table[four(idx[span, base + first + u]), :] for u in range(8)]
                    for at, row in zip(ats, rows):
                        stage[at, :] = row

        sub = 32
        lane = lax.broadcasted_iota(jnp.int32, (sub, LANES), 1)
        low = lane < 72

        @pl.loop(0, TILE, step=sub)
        def _(r0):
            r0 = pl.multiple_of(r0, sub)
            here = pl.ds(pl.multiple_of(base + r0, sub), sub)
            s, r, t = (
                [st[column(r0, j, sub), :] for j in range(4)]
                for st in (st_s, st_r, st_t)
            )
            re0 = s[0] * r[0] - s[2] * r[2]
            re1 = s[1] * r[1] - s[3] * r[3]
            im0 = s[0] * r[2] + s[2] * r[0]
            im1 = s[1] * r[3] + s[3] * r[1]
            prod = (re0, re1, im0, im1)
            score = jnp.sum(re0 * t[0] + re1 * t[1] + im0 * t[2] + im1 * t[3], -1, keepdims=True)
            row = lax.broadcasted_iota(jnp.int32, (sub, 1), 0) + (base + r0)
            weight = jnp.where(row < count, 1.0, 0.0)
            grad = -(0.5 - 0.5 * jnp.tanh(0.5 * score)) * weight
            for j in range(4):
                src_ref[0, here, j * LANES : (j + 1) * LANES] = s[j]
                rel_ref[0, here, j * LANES : (j + 1) * LANES] = r[j]
                tgt_ref[0, here, j * LANES : (j + 1) * LANES] = grad * t[j]
                gt_ref[column(base + r0, j, sub), :] = grad * prod[j]
            r_a = pltpu.roll(im0, 72, 1)
            r_b = pltpu.roll(im1, 72, 1)
            natural = (
                re0, jnp.where(low, re1, r_a), jnp.where(low, r_a, r_b), jnp.where(low, r_b, 0.0),
            )
            for j in range(4):
                p_ref[0, here, j * LANES : (j + 1) * LANES] = natural[j].astype(BF16)

        width = pt_ref.shape[1]
        here = pl.ds(base, TILE)
        for j in range(4):
            size = min(LANES, width - j * LANES)
            x = p_ref[0, here, j * LANES : (j + 1) * LANES].T
            pt_ref[0, j * LANES : j * LANES + size, here] = x[:size]
        return 0

    lax.fori_loop(0, tiles_of(count), one_tile, 0)


def edges(src_idx, rel_idx, tgt_idx, live, left4, rel4, right4, width):
    spans, length = src_idx.shape
    row_spec = pl.BlockSpec((1, length, 512), lambda s, *_: (s, 0, 0))
    rows_f32 = jax.ShapeDtypeStruct((spans, length, 512), F32)
    return pl.pallas_call(
        edge_kernel,
        grid_spec=pltpu.PrefetchScalarGridSpec(
            num_scalar_prefetch=4,
            grid=(spans,),
            in_specs=[whole(left4.shape), whole(rel4.shape), whole(right4.shape)],
            out_specs=[
                row_spec,
                pl.BlockSpec((1, width, length), lambda s, *_: (s, 0, 0)),
                row_spec,
                row_spec,
                row_spec,
                pl.BlockSpec((PITCH * length, LANES), lambda s, *_: (s, 0)),
            ],
            scratch_shapes=[pltpu.VMEM((PITCH * TILE, LANES), F32)] * 3,
        ),
        out_shape=[
            jax.ShapeDtypeStruct((spans, length, 512), BF16),
            jax.ShapeDtypeStruct((spans, width, length), BF16),
            rows_f32,
            rows_f32,
            rows_f32,
            jax.ShapeDtypeStruct((spans * PITCH * length, LANES), F32),
        ],
        compiler_params=params(),
        cost_estimate=cost(0, 300e6),
        name="edges",
    )(src_idx, rel_idx, tgt_idx, live, left4, rel4, right4)


def target_kernel(tgt_idx, live, gt_ref, gr4):
    span = pl.program_id(0)

    @pl.when(span == 0)
    def _():
        gr4[...] = jnp.zeros(gr4.shape, F32)

    def some(n, _):
        r0 = pl.multiple_of(n * GROUP, GROUP)
        for v in range(0, GROUP, 2):
            add_rows(((tgt_idx, gr4, gt_ref),), span, r0 + v, r0, v, 2)
        return 0

    lax.fori_loop(0, tiles_of(live[span]) * (TILE // GROUP), some, 0)


def target_grads(tgt_idx, live, gt, size):
    spans, length = tgt_idx.shape
    return pl.pallas_call(
        target_kernel,
        grid_spec=pltpu.PrefetchScalarGridSpec(
            num_scalar_prefetch=2,
            grid=(spans,),
            in_specs=[pl.BlockSpec((PITCH * length, LANES), lambda s, *_: (s, 0))],
            out_specs=whole((size, LANES)),
        ),
        out_shape=jax.ShapeDtypeStruct((size, LANES), F32),
        compiler_params=params(),
        cost_estimate=cost(0, 100e6),
        name="target_grads",
    )(tgt_idx, live, gt)


def later_span_kernel(live, neg_ref, p_ref, pt_ref, _, *refs, first):
    span_kernel(live, neg_ref, p_ref, pt_ref, *refs, first=first)


def span_kernel(live, neg_ref, p_ref, pt_ref, gp_ref, gn_ref, negs, acc, *, first):
    shards, width, npp = neg_ref.shape
    count = live[first + pl.program_id(0)]
    for o in range(shards):
        negs[:width, o * npp : (o + 1) * npp] = neg_ref[o]
    negs[width:, :] = jnp.zeros((negs.shape[0] - width, shards * npp), BF16)
    acc[...] = jnp.zeros(acc.shape, F32)

    def step(t, _):
        base = pl.multiple_of(t * TILE, TILE)
        here = pl.ds(base, TILE)
        n = negs[...]
        row = lax.broadcasted_iota(jnp.int32, (TILE, 1), 0) + base
        half = jnp.where(row < count, 0.5, 0.0)
        scores = jnp.dot(p_ref[0, here, :], n, preferred_element_type=F32)
        ng = (half * jnp.tanh(0.5 * scores) + half).astype(BF16)
        gp_ref[0, here, :] = lax.dot_general(ng, n, (((1,), (1,)), ((), ())), preferred_element_type=F32)
        acc[...] += jnp.dot(pt_ref[0, :, here], ng, preferred_element_type=F32)
        return 0

    lax.fori_loop(0, tiles_of(count), step, 0)
    for o in range(shards):
        gn_ref[o] = acc[:, o * npp : (o + 1) * npp].astype(BF16)


def span_grads(live, negatives, p, pt, grad_products, first, count):
    shards, width, lanes = negatives.shape
    npp = lanes // count
    spans, length, _ = p.shape
    later = grad_products is not None
    return pl.pallas_call(
        functools.partial(later_span_kernel if later else span_kernel, first=first),
        grid_spec=pltpu.PrefetchScalarGridSpec(
            num_scalar_prefetch=1,
            grid=(count,),
            in_specs=[
                pl.BlockSpec((shards, width, npp), lambda s, *_: (0, 0, s)),
                pl.BlockSpec((1, length, 512), lambda s, *_: (s + first, 0, 0)),
                pl.BlockSpec((1, width, length), lambda s, *_: (s + first, 0, 0)),
            ]
            + ([pl.BlockSpec(memory_space=pl.ANY)] if later else []),
            out_specs=[
                pl.BlockSpec((1, length, 512), lambda s, *_: (s + first, 0, 0)),
                pl.BlockSpec((shards, width, npp), lambda s, *_: (0, 0, s)),
            ],
            scratch_shapes=[
                pltpu.VMEM((512, shards * npp), BF16),
                pltpu.VMEM((width, shards * npp), F32),
            ],
        ),
        out_shape=[
            jax.ShapeDtypeStruct((spans, length, 512), F32),
            jax.ShapeDtypeStruct((shards, width, lanes), BF16),
        ],
        input_output_aliases={4: 0} if later else {},
        compiler_params=params(),
        cost_estimate=cost(count * 6 * length * 512 * shards * npp, 8 * count * length * 512),
        name="span_grads",
    )(live, negatives, p, pt, *([grad_products] if later else []))


def source_kernel(
    src_idx, rel_idx, live, gp_ref, src_ref, rel_ref, tgt_ref, gl_in, gk_in, gl4, gk4, st_s, st_r, *, first
):
    span = pl.program_id(0)

    @pl.when(span == 0)
    def _():
        if gl_in is None:
            gl4[...] = jnp.zeros(gl4.shape, F32)
            gk4[...] = jnp.zeros(gk4.shape, F32)
        else:
            gl4[...] = gl_in[...]
            gk4[...] = gk_in[...]

    def one_tile(tile, _):
        base = pl.multiple_of(tile * TILE, TILE)
        sub = 32
        lane = lax.broadcasted_iota(jnp.int32, (sub, LANES), 1)
        low = lane < 72

        @pl.loop(0, TILE, step=sub)
        def _(r0):
            r0 = pl.multiple_of(r0, sub)
            here = pl.ds(pl.multiple_of(base + r0, sub), sub)
            n, s, r, t = (
                [ref[0, here, j * LANES : (j + 1) * LANES] for j in range(4)]
                for ref in (gp_ref, src_ref, rel_ref, tgt_ref)
            )
            re0 = n[0] + t[0]
            re1 = n[1] + t[1]
            im0 = pltpu.roll(jnp.where(low, n[2], n[1]), 56, 1) + t[2]
            im1 = pltpu.roll(jnp.where(low, n[3], n[2]), 56, 1) + t[3]
            for other, stage in ((r, st_s), (s, st_r)):
                grads = (
                    re0 * other[0] + im0 * other[2],
                    re1 * other[1] + im1 * other[3],
                    im0 * other[0] - re0 * other[2],
                    im1 * other[1] - re1 * other[3],
                )
                for j in range(4):
                    stage[column(r0, j, sub), :] = grads[j]

        @pl.loop(0, TILE, step=GROUP)
        def _(r0):
            for v in range(0, GROUP, 2):
                add_rows(((src_idx, gl4, st_s), (rel_idx, gk4, st_r)), first + span, base + r0 + v, r0, v, 2)

        return 0

    lax.fori_loop(0, tiles_of(live[first + span]), one_tile, 0)


def first_source_kernel(src_idx, rel_idx, live, gp, src, rel, tgt, gl4, gk4, st_s, st_r, *, first):
    source_kernel(src_idx, rel_idx, live, gp, src, rel, tgt, None, None, gl4, gk4, st_s, st_r, first=first)


def source_grads(src_idx, rel_idx, live, gp, src, rel, tgt, totals, sizes, first, count):
    spans, length = src_idx.shape
    row_spec = pl.BlockSpec((1, length, 512), lambda s, *_: (s + first, 0, 0))
    outs = [whole((n, LANES)) for n in sizes]
    body = first_source_kernel if totals is None else source_kernel
    return pl.pallas_call(
        functools.partial(body, first=first),
        grid_spec=pltpu.PrefetchScalarGridSpec(
            num_scalar_prefetch=3,
            grid=(count,),
            in_specs=[row_spec] * 4 + ([] if totals is None else outs),
            out_specs=outs,
            scratch_shapes=[pltpu.VMEM((PITCH * TILE, LANES), F32)] * 2,
        ),
        out_shape=[jax.ShapeDtypeStruct((n, LANES), F32) for n in sizes],
        compiler_params=params(),
        cost_estimate=cost(0, 30e6 * count),
        name="source_grads",
    )(src_idx, rel_idx, live, gp, src, rel, tgt, *(totals or ()))


def joined(ref, b, width):
    return [
        ref[pl.ds(4 * LANES * b + j, LANES, stride=4), :].T[:size]
        for j, (_, size) in enumerate(parts_of(width))
    ]


def relation_kernel(g_ref, t_ref, s_ref, _, o_ref, *, width, rows, spare):
    grads = [g_ref[pl.ds(j, rows, stride=4), :] for j in range(4)]
    square = grads[0] * grads[0] + grads[1] * grads[1] + grads[2] * grads[2] + grads[3] * grads[3]
    state = s_ref[...] + jnp.sum(square, -1, keepdims=True) * (1.0 / width)
    scale = LEARN_RATE / (jnp.sqrt(state) + EPSILON)
    lane = lax.broadcasted_iota(jnp.int32, (rows, LANES), 1)
    for j in range(4):
        new = t_ref[pl.ds(j, rows, stride=4), :] - grads[j] * scale
        if j == 1:
            new = jnp.where(lane == spare, state, new)
        o_ref[pl.ds(j, rows, stride=4), :] = new


def update_relations(g4, t4, state, held, width):
    rows = state.shape[0]
    spare = parts_of(width)[1][1]
    full = [pl.BlockSpec(x.shape, lambda: (0, 0)) for x in (g4, t4, state)]
    return pl.pallas_call(
        functools.partial(relation_kernel, width=width, rows=rows, spare=spare),
        in_specs=full + [pl.BlockSpec(memory_space=pl.ANY)],
        out_specs=full[0],
        out_shape=jax.ShapeDtypeStruct(g4.shape, F32),
        compiler_params=params(),
        cost_estimate=cost(0, 3e6),
        name="update_relations",
    )(g4, t4, state, held)


def join_kernel(g_ref, o_ref, s_ref, *, width, cols):
    spare = parts_of(width)[1][1]
    for b in range(cols // LANES):
        here = slice(b * LANES, min((b + 1) * LANES, o_ref.shape[1]))
        count = here.stop - here.start
        for j, (start, size) in enumerate(parts_of(width)):
            x = g_ref[pl.ds(4 * LANES * b + j, LANES, stride=4), :].T
            o_ref[start : start + size, here] = x[:size, :count]
            if j == 1:
                s_ref[:, here] = x[spare : spare + 1, :count]


def join_relations(rows4, width, kinds):
    return pl.pallas_call(
        functools.partial(join_kernel, width=width, cols=rows4.shape[0] // 4),
        in_specs=[pl.BlockSpec(rows4.shape, lambda: (0, 0))],
        out_specs=[pl.BlockSpec((width, kinds), lambda: (0, 0)), pl.BlockSpec((1, kinds), lambda: (0, 0))],
        out_shape=[jax.ShapeDtypeStruct((width, kinds), F32), jax.ShapeDtypeStruct((1, kinds), F32)],
        compiler_params=params(),
        cost_estimate=cost(0, 4 * kinds * (width + 512)),
        name="join_relations",
    )(rows4)


def update(grad, t_ref, s_ref, q_ref, m_ref, start, size):
    here = slice(start, start + size)
    width = t_ref.shape[0]
    state = s_ref[0:1, here] + jnp.sum(grad * grad, 0, keepdims=True) * (1.0 / width)
    new = t_ref[:, here] - grad * (LEARN_RATE / (jnp.sqrt(state) + EPSILON))
    top = jnp.max(jnp.abs(new), 0, keepdims=True)
    code = new * (CODE / jnp.maximum(top, 1e-30))
    q_ref[:, here] = jnp.round(code).astype(jnp.int32).astype(jnp.int16)
    m_ref[0:1, here] = top
    m_ref[1:2, here] = state


def left_kernel(g_ref, t_ref, s_ref, q_ref, m_ref, *, width, cols):
    for b in range(cols // LANES):
        grad = jnp.concatenate(joined(g_ref, b, width), 0)
        update(grad, t_ref, s_ref, q_ref, m_ref, b * LANES, LANES)


def coded_shapes(width, rows):
    return [jax.ShapeDtypeStruct((width, rows), jnp.int16), jax.ShapeDtypeStruct((2, rows), F32)]


def update_left(g4, table_t, state, cols, start, blocks):
    width, rows = table_t.shape
    return pl.pallas_call(
        functools.partial(left_kernel, width=width, cols=cols),
        grid=(blocks,),
        in_specs=[
            pl.BlockSpec((4 * cols, LANES), lambda i: (i + start, 0)),
            pl.BlockSpec((width, cols), lambda i: (0, i + start)),
            pl.BlockSpec((1, cols), lambda i: (0, i + start)),
        ],
        out_specs=[pl.BlockSpec((width, cols), lambda i: (0, i)), pl.BlockSpec((2, cols), lambda i: (0, i))],
        out_shape=coded_shapes(width, blocks * cols),
        compiler_params=params(),
        cost_estimate=cost(0, 10 * blocks * cols * width),
        name="update_left",
    )(g4, table_t, state)


def negative_sum(acc, idx_ref, b_ref, cols, step, start=0):
    shards, _, lanes = b_ref.shape
    row = lax.broadcasted_iota(jnp.int16, (cols, step), 0)
    one, zero = jnp.ones((), BF16), jnp.zeros((), BF16)
    for q in range(shards):
        for k in range(0, lanes, step):
            idx = (idx_ref[q, :, k : k + step] - (pl.program_id(0) + start) * cols).astype(jnp.int16)
            hot = jnp.where(row == idx, one, zero)
            acc += lax.dot_general(
                b_ref[q, :, k : k + step], hot, (((1,), (1,)), ((), ())), preferred_element_type=F32
            )
    return acc


def first_spread_kernel(idx_ref, b_ref, o_ref, *, cols, step):
    o_ref[...] = negative_sum(jnp.zeros(o_ref.shape, F32), idx_ref, b_ref, cols, step)


def spread_kernel(g_ref, g4_ref, idx_ref, b_ref, o_ref, *, cols, step):
    o_ref[...] = negative_sum(g_ref[...], idx_ref, b_ref, cols, step)
    width = o_ref.shape[0]
    for b in range(cols // LANES):
        for (start, size), x in zip(parts_of(width), joined(g4_ref, b, width)):
            o_ref[start : start + size, b * LANES : (b + 1) * LANES] += x


def spread_update_kernel(g_ref, idx_ref, b_ref, t_ref, s_ref, q_ref, m_ref, acc, *, cols, step, start):
    acc[...] = negative_sum(g_ref[...], idx_ref, b_ref, cols, step, start)
    for b in range(cols // LANES):
        update(acc[:, b * LANES : (b + 1) * LANES], t_ref, s_ref, q_ref, m_ref, b * LANES, LANES)


def spread(grads, idx, returned, rows, cols):
    shards, width, lanes = returned.shape
    block = pl.BlockSpec((width, cols), lambda i: (0, i))
    return pl.pallas_call(
        functools.partial(
            spread_kernel if grads else first_spread_kernel,
            cols=cols, step=2 * LANES if lanes % 256 == 0 else LANES,
        ),
        grid=(rows // cols,),
        in_specs=([block, pl.BlockSpec((4 * cols, LANES), lambda i: (i, 0))] if grads else [])
        + [whole(idx.shape), whole(returned.shape)],
        out_specs=block,
        out_shape=jax.ShapeDtypeStruct((width, rows), F32),
        compiler_params=params(),
        cost_estimate=cost(2 * width * rows * shards * lanes, 8 * width * rows),
        name="spread",
    )(*grads, idx, returned)


def spread_update(grad_t, idx, returned, table_t, state, cols, start, blocks):
    width, rows = grad_t.shape
    shards, _, lanes = returned.shape
    here = pl.BlockSpec((width, cols), lambda i: (0, i + start))
    return pl.pallas_call(
        functools.partial(
            spread_update_kernel, cols=cols, step=2 * LANES if lanes % 256 == 0 else LANES, start=start
        ),
        grid=(blocks,),
        in_specs=[
            here, whole(idx.shape), whole(returned.shape), here, pl.BlockSpec((1, cols), lambda i: (0, i + start)),
        ],
        out_specs=[pl.BlockSpec((width, cols), lambda i: (0, i)), pl.BlockSpec((2, cols), lambda i: (0, i))],
        out_shape=coded_shapes(width, blocks * cols),
        scratch_shapes=[pltpu.VMEM((width, cols), F32)],
        compiler_params=params(),
        cost_estimate=cost(2 * width * blocks * cols * shards * lanes, 8 * width * blocks * cols),
        name="spread_update",
    )(grad_t, idx, returned, table_t, state)


def decode_kernel(m_ref, *refs, ways):
    code = sum(ref[...].astype(jnp.int32) for ref in refs[:ways])
    refs[-1][...] = code.astype(F32) * (m_ref[0:1, :] * (1.0 / CODE))


def decode(codes, meta, rows, cols, start, table_t):
    width, count = codes[0].shape
    ways = len(codes)
    block = pl.BlockSpec((width, cols), lambda i: (0, i))
    return pl.pallas_call(
        functools.partial(decode_kernel, ways=ways),
        grid=(count // cols,),
        in_specs=[pl.BlockSpec((2, cols), lambda i: (0, i + start))]
        + [block] * ways
        + ([] if table_t is None else [pl.BlockSpec(memory_space=pl.ANY)]),
        out_specs=pl.BlockSpec((width, cols), lambda i: (0, i + start)),
        out_shape=jax.ShapeDtypeStruct((width, rows), F32),
        input_output_aliases={} if table_t is None else {1 + ways: 0},
        compiler_params=params(),
        cost_estimate=cost(0, 6 * width * count),
        name="decode",
    )(meta, *codes, *([] if table_t is None else [table_t]))


def passed_along(block, axis, distance):
    devices = range(lax.axis_size(axis))
    route = [((i - distance) % len(devices), i) for i in devices]
    return lax.ppermute(block, axis, route)


def corner_senders(n):
    return [i for i in range(n) if i % 4 == 1]


def handed_over(halves, held, before_meta=()):
    (first, meta_a), (second, meta_b) = halves
    n = lax.axis_size("grp")
    turning = corner_senders(n)
    there = lax.ppermute(first, "grp", [(i, (i + ROUND - 1) % n) for i in turning])
    straight = lax.ppermute(first, "grp", [(i, (i + ROUND) % n) for i in range(n) if i not in turning])
    other = passed_along(second, "grp", ROUND)
    meta = after(jnp.concatenate([meta_a, meta_b], 1), *before_meta)
    meta = passed_along(meta, "grp", ROUND)
    here = lax.ppermute(
        after(there, *held), "grp", [((i + ROUND - 1) % n, (i + ROUND) % n) for i in turning]
    )
    return ((straight, here), (other,)), meta, there


def decoded(arrived, rows, cols, held):
    table, start = None, 0
    halves, meta = arrived[:2]
    for codes in halves:
        table = decode((after(codes[0], *held), *codes[1:]), meta, rows, cols, start, table)
        start += codes[0].shape[1] // cols
    return table, meta[1]


def exchanged(blocks):
    return lax.all_to_all(blocks, "shard", split_axis=0, concat_axis=0, tiled=True)


def after(value, *others):
    return lax.optimization_barrier((value, *others))[0]


def local(
    left_table,
    right_table,
    left_state,
    right_state,
    relations,
    relation_state,
    source_rows,
    relation_ids,
    target_rows,
    negative_rows,
    span_sizes,
):
    shards = lax.axis_size("shard")
    spans, span_len = source_rows.shape
    neg_per = negative_rows.shape[1] // shards
    npp = round_up(neg_per, LANES)
    rows, width = left_table.shape
    kinds = relations.shape[0]
    kinds_up = round_up(kinds, LANES)
    length = round_up(span_len, TILE)

    left_t, right_t, rel_t = left_table.T, right_table.T, relations.T
    live = span_sizes[0]

    ids = negative_rows.reshape(spans, shards, neg_per)
    ids = jnp.pad(ids, ((0, 0), (0, 0), (0, npp - neg_per)), constant_values=-1)
    asked = lax.all_to_all(ids.transpose(1, 0, 2), "shard", split_axis=0, concat_axis=0, tiled=True)
    asked_lanes = asked.reshape(shards, spans, 1, npp)

    src_idx, rel_idx, tgt_idx = (
        jnp.pad(a, ((0, 0), (0, length - span_len))) for a in (source_rows, relation_ids, target_rows)
    )

    third = -(-spans // 3)
    (c0, c1, c2) = [(a, min(third, spans - a)) for a in range(0, spans, third)]

    served0 = serve(asked_lanes, right_t, *c0)
    fetched0 = exchanged(served0)
    served1 = serve(after(asked_lanes, served0), right_t, *c1)
    served2 = serve(after(asked_lanes, served1), right_t, *c2)
    left4 = split_rows(after(left_t, served2), 512)
    right4 = split_rows(after(right_t, served2), 512)
    rel4 = split_rows(after(rel_t, served2), kinds_up)

    fetched1 = exchanged(after(served1, left4, right4, rel4))
    p, pt, src, rel, tgt, gt = edges(
        src_idx, rel_idx, tgt_idx, live, after(left4, fetched0), rel4, right4, width
    )

    fetched2 = exchanged(after(served2, p))
    gp, gn0 = span_grads(live, after(fetched0, fetched1), p, pt, None, *c0)
    gp, gn1 = span_grads(live, fetched1, p, pt, gp, *c1)
    sizes = (4 * rows, 4 * kinds_up)
    sums = functools.partial(source_grads, src_idx, rel_idx, live)
    totals = sums(gp, src, rel, tgt, None, sizes, *c0)

    returned0 = exchanged(after(gn0, totals[1], fetched2))
    gp, gn2 = span_grads(live, fetched2, p, pt, after(gp, totals[1]), *c2)
    gl4, gk4 = sums(gp, src, rel, tgt, totals, sizes, c1[0], c1[1] + c2[1])

    returned1 = exchanged(after(gn1, gk4, returned0))
    rel_total4 = lax.psum_scatter(gk4, "grp", scatter_dimension=0, tiled=True)
    lanes0, lanes1, lanes2 = (
        asked[:, a : a + n].reshape(shards, 1, n * npp) for a, n in (c0, c1, c2)
    )
    blocks = rows // 512
    halves = ((0, blocks // 2), (blocks // 2, blocks - blocks // 2))
    left_in = after(left_t, gk4)
    coded_left = [tuple(update_left(gl4, left_in, left_state[None], 512, *half)) for half in halves]
    left_sent = tuple(c[1] for c in coded_left)
    gr4 = target_grads(tgt_idx, live, after(gt, *left_sent), 4 * rows)
    moved_left = handed_over(coded_left, (gr4,))

    returned2 = exchanged(after(gn2, gr4, moved_left[2], moved_left[0][0][0], returned1))
    rel_sum4 = lax.psum(after(rel_total4, gr4), "shard")
    grad_right = spread((), lanes0, after(returned0, gr4), rows, 512)
    grad_right = spread((grad_right, gr4), lanes1, returned1, rows, 512)
    grad_right = after(grad_right, *moved_left[0][0], *moved_left[0][1], moved_left[1])

    coded = []
    for half in halves:
        coded.append(
            tuple(spread_update(grad_right, lanes2, returned2, right_t, right_state[None], 512, *half))
        )
        grad_right = after(grad_right, coded[-1][1])
    new_left, new_left_state = decoded(moved_left, rows, 512, (coded[1][1],))
    slice_rows = kinds_up // lax.axis_size("grp")
    place = lax.axis_index("grp") * slice_rows
    own_rel4 = lax.dynamic_slice(rel4, (4 * place, 0), (4 * slice_rows, LANES))
    own_state = lax.dynamic_slice(
        jnp.pad(relation_state, (0, kinds_up - kinds))[:, None], (place, 0), (slice_rows, 1)
    )
    new_rel4 = update_relations(rel_sum4, own_rel4, own_state, coded[1][1], width)
    new_rel4 = lax.all_gather(new_rel4, "grp", axis=0, tiled=True)
    new_rel_t, new_relation_state = join_relations(new_rel4, width, kinds)
    moved_right = handed_over(coded, (coded[1][1],), (new_rel_t,))
    new_right, new_right_state = decoded(moved_right, rows, 512, (new_left, new_rel_t))
    return (new_left.T, new_left_state, new_right.T, new_right_state, new_rel_t.T, new_relation_state[0])


def solution(mesh):
    rows2, rows1 = P(("grp", "shard"), None), P(("grp", "shard"))
    return jax.shard_map(
        local,
        mesh=mesh,
        in_specs=(rows2, rows2, rows1, rows1, P(), P(), rows2, rows2, rows2, rows2, rows2),
        out_specs=(rows2, rows1, rows2, rows1, P(), P()),
        check_vma=False,
    )
```

```python
import functools

import jax
import jax.numpy as jnp
from jax import lax
from jax.experimental import pallas as pl
from jax.experimental.pallas import tpu as pltpu
from jax.sharding import PartitionSpec as P

ROUND = 5
LEARN_RATE = 0.1
EPSILON = 1e-08
LANES = 128
TILE = 256
GROUP = 32
PITCH = 5
CODE = 32767.0
VMEM_LIMIT = 58 * 1024 * 1024
F32 = jnp.float32
BF16 = jnp.bfloat16


def round_up(n, m):
    return -(-n // m) * m


def params(**kw):
    return pltpu.CompilerParams(vmem_limit_bytes=VMEM_LIMIT, **kw)


def cost(flops, nbytes):
    return pl.CostEstimate(flops=int(flops), bytes_accessed=int(nbytes), transcendentals=0)


def whole(shape):
    return pl.BlockSpec(shape, lambda *_: (0,) * len(shape), pipeline_mode=pl.Buffered(1))


def parts_of(width):
    half = width // 2
    rest = half - LANES
    return ((0, LANES), (LANES, rest), (half, LANES), (half + LANES, rest))


def split_kernel(t_ref, o_ref, *, width, cols):
    for b in range(cols // LANES):
        for j, (start, size) in enumerate(parts_of(width)):
            x = t_ref[start : start + size, b * LANES : (b + 1) * LANES]
            if size < LANES:
                x = jnp.concatenate([x, jnp.zeros((LANES - size, LANES), F32)], 0)
            o_ref[pl.ds(4 * LANES * b + j, LANES, stride=4), :] = x.T


def split_rows(table_t, cols):
    width, rows = table_t.shape
    rows = round_up(rows, cols)
    return pl.pallas_call(
        functools.partial(split_kernel, width=width, cols=cols),
        grid=(rows // cols,),
        in_specs=[pl.BlockSpec((width, cols), lambda i: (0, i))],
        out_specs=pl.BlockSpec((4 * cols, LANES), lambda i: (i, 0)),
        out_shape=jax.ShapeDtypeStruct((4 * rows, LANES), F32),
        compiler_params=params(),
        cost_estimate=cost(0, 4 * rows * (width + 512)),
        name="split_rows",
    )(table_t)


def serve_kernel(idx_ref, t_ref, o_ref, tb, *, rows, step):
    @pl.when((pl.program_id(0) == 0) & (pl.program_id(1) == 0))
    def _():
        for k in range(0, rows, step):
            tb[:, k : k + step] = t_ref[:, k : k + step].astype(BF16)

    idx = idx_ref[0, 0].astype(jnp.int16)
    lanes = idx.shape[-1]
    row = lax.broadcasted_iota(jnp.int16, (step, lanes), 0)
    one, zero = jnp.ones((), BF16), jnp.zeros((), BF16)
    acc = jnp.zeros((t_ref.shape[0], lanes), F32)
    for k in range(0, rows, step):
        hot = jnp.where(row == idx - k, one, zero)
        acc += jnp.dot(tb[:, k : k + step], hot, preferred_element_type=F32)
    o_ref[0] = acc.astype(BF16)


def serve(asked, table_t, first, count):
    shards, spans, _, npp = asked.shape
    width, rows = table_t.shape
    return pl.pallas_call(
        functools.partial(serve_kernel, rows=rows, step=512),
        grid=(shards, count),
        in_specs=[
            pl.BlockSpec((1, 1, 1, npp), lambda q, s: (q, s + first, 0, 0)),
            whole((width, rows)),
        ],
        out_specs=pl.BlockSpec((1, width, npp), lambda q, s: (q, 0, s)),
        out_shape=jax.ShapeDtypeStruct((shards, width, count * npp), BF16),
        scratch_shapes=[pltpu.VMEM((width, rows), BF16)],
        compiler_params=params(),
        cost_estimate=cost(2 * width * rows * shards * count * npp, 4 * width * rows),
        name="serve",
    )(asked, table_t)


def four(i):
    return pl.ds(pl.multiple_of(4 * i, 4), 4)


def staged(first, u):
    return pl.ds(pl.multiple_of(PITCH * first, 8) + PITCH * u, 4)


def column(first, j, size):
    return pl.ds(pl.multiple_of(PITCH * first, 8) + j, size, stride=PITCH)


def add_rows(jobs, span, edge, first, at, n):
    done = []
    for idx, total, stage in jobs:
        ids = [idx[span, edge + u] for u in range(n)]
        grads = [stage[staged(first, at + u), :] for u in range(n)]
        sums = [total[four(i), :] for i in ids]
        for k in range(n):
            new = sums[k] + grads[k]
            for j in range(k):
                new += grads[j] * jnp.where(ids[j] == ids[k], 1.0, 0.0)
            done.append((total, ids[k], new))
    for total, i, new in done:
        total[four(i), :] = new


def tiles_of(count):
    return (count + TILE - 1) // TILE


def edge_kernel(
    src_idx, rel_idx, tgt_idx, live,
    left4, rel4, right4,
    p_ref, pt_ref, src_ref, rel_ref, tgt_ref, gt_ref,
    st_s, st_r, st_t,
):
    span = pl.program_id(0)
    count = live[span]

    def one_tile(tile, _):
        base = pl.multiple_of(tile * TILE, TILE)

        @pl.loop(0, TILE, step=GROUP)
        def _(r0):
            for v in range(0, GROUP, 8):
                first = r0 + v
                ats = [staged(first, u) for u in range(8)]
                for idx, table, stage in (
                    (src_idx, left4, st_s), (rel_idx, rel4, st_r), (tgt_idx, right4, st_t),
                ):
                    rows = [table[four(idx[span, base + first + u]), :] for u in range(8)]
                    for at, row in zip(ats, rows):
                        stage[at, :] = row

        sub = 32
        lane = lax.broadcasted_iota(jnp.int32, (sub, LANES), 1)
        low = lane < 72

        @pl.loop(0, TILE, step=sub)
        def _(r0):
            r0 = pl.multiple_of(r0, sub)
            here = pl.ds(pl.multiple_of(base + r0, sub), sub)
            s, r, t = (
                [st[column(r0, j, sub), :] for j in range(4)]
                for st in (st_s, st_r, st_t)
            )
            re0 = s[0] * r[0] - s[2] * r[2]
            re1 = s[1] * r[1] - s[3] * r[3]
            im0 = s[0] * r[2] + s[2] * r[0]
            im1 = s[1] * r[3] + s[3] * r[1]
            prod = (re0, re1, im0, im1)
            score = jnp.sum(re0 * t[0] + re1 * t[1] + im0 * t[2] + im1 * t[3], -1, keepdims=True)
            row = lax.broadcasted_iota(jnp.int32, (sub, 1), 0) + (base + r0)
            weight = jnp.where(row < count, 1.0, 0.0)
            grad = -(0.5 - 0.5 * jnp.tanh(0.5 * score)) * weight
            for j in range(4):
                src_ref[0, here, j * LANES : (j + 1) * LANES] = s[j]
                rel_ref[0, here, j * LANES : (j + 1) * LANES] = r[j]
                tgt_ref[0, here, j * LANES : (j + 1) * LANES] = grad * t[j]
                gt_ref[column(base + r0, j, sub), :] = grad * prod[j]
            r_a = pltpu.roll(im0, 72, 1)
            r_b = pltpu.roll(im1, 72, 1)
            natural = (
                re0, jnp.where(low, re1, r_a), jnp.where(low, r_a, r_b), jnp.where(low, r_b, 0.0),
            )
            for j in range(4):
                p_ref[0, here, j * LANES : (j + 1) * LANES] = natural[j].astype(BF16)

        width = pt_ref.shape[1]
        here = pl.ds(base, TILE)
        for j in range(4):
            size = min(LANES, width - j * LANES)
            x = p_ref[0, here, j * LANES : (j + 1) * LANES].T
            pt_ref[0, j * LANES : j * LANES + size, here] = x[:size]
        return 0

    lax.fori_loop(0, tiles_of(count), one_tile, 0)


def edges(src_idx, rel_idx, tgt_idx, live, left4, rel4, right4, width):
    spans, length = src_idx.shape
    row_spec = pl.BlockSpec((1, length, 512), lambda s, *_: (s, 0, 0))
    rows_f32 = jax.ShapeDtypeStruct((spans, length, 512), F32)
    return pl.pallas_call(
        edge_kernel,
        grid_spec=pltpu.PrefetchScalarGridSpec(
            num_scalar_prefetch=4,
            grid=(spans,),
            in_specs=[whole(left4.shape), whole(rel4.shape), whole(right4.shape)],
            out_specs=[
                row_spec,
                pl.BlockSpec((1, width, length), lambda s, *_: (s, 0, 0)),
                row_spec,
                row_spec,
                row_spec,
                pl.BlockSpec((PITCH * length, LANES), lambda s, *_: (s, 0)),
            ],
            scratch_shapes=[pltpu.VMEM((PITCH * TILE, LANES), F32)] * 3,
        ),
        out_shape=[
            jax.ShapeDtypeStruct((spans, length, 512), BF16),
            jax.ShapeDtypeStruct((spans, width, length), BF16),
            rows_f32,
            rows_f32,
            rows_f32,
            jax.ShapeDtypeStruct((spans * PITCH * length, LANES), F32),
        ],
        compiler_params=params(),
        cost_estimate=cost(0, 300e6),
        name="edges",
    )(src_idx, rel_idx, tgt_idx, live, left4, rel4, right4)


def target_kernel(tgt_idx, live, gt_ref, gr4):
    span = pl.program_id(0)

    @pl.when(span == 0)
    def _():
        gr4[...] = jnp.zeros(gr4.shape, F32)

    def some(n, _):
        r0 = pl.multiple_of(n * GROUP, GROUP)
        for v in range(0, GROUP, 2):
            add_rows(((tgt_idx, gr4, gt_ref),), span, r0 + v, r0, v, 2)
        return 0

    lax.fori_loop(0, tiles_of(live[span]) * (TILE // GROUP), some, 0)


def target_grads(tgt_idx, live, gt, size):
    spans, length = tgt_idx.shape
    return pl.pallas_call(
        target_kernel,
        grid_spec=pltpu.PrefetchScalarGridSpec(
            num_scalar_prefetch=2,
            grid=(spans,),
            in_specs=[pl.BlockSpec((PITCH * length, LANES), lambda s, *_: (s, 0))],
            out_specs=whole((size, LANES)),
        ),
        out_shape=jax.ShapeDtypeStruct((size, LANES), F32),
        compiler_params=params(),
        cost_estimate=cost(0, 100e6),
        name="target_grads",
    )(tgt_idx, live, gt)


def later_span_kernel(live, neg_ref, p_ref, pt_ref, _, *refs, first):
    span_kernel(live, neg_ref, p_ref, pt_ref, *refs, first=first)


def span_kernel(live, neg_ref, p_ref, pt_ref, gp_ref, gn_ref, negs, acc, *, first):
    shards, width, npp = neg_ref.shape
    count = live[first + pl.program_id(0)]
    for o in range(shards):
        negs[:width, o * npp : (o + 1) * npp] = neg_ref[o]
    negs[width:, :] = jnp.zeros((negs.shape[0] - width, shards * npp), BF16)
    acc[...] = jnp.zeros(acc.shape, F32)

    def step(t, _):
        base = pl.multiple_of(t * TILE, TILE)
        here = pl.ds(base, TILE)
        n = negs[...]
        row = lax.broadcasted_iota(jnp.int32, (TILE, 1), 0) + base
        half = jnp.where(row < count, 0.5, 0.0)
        scores = jnp.dot(p_ref[0, here, :], n, preferred_element_type=F32)
        ng = (half * jnp.tanh(0.5 * scores) + half).astype(BF16)
        gp_ref[0, here, :] = lax.dot_general(ng, n, (((1,), (1,)), ((), ())), preferred_element_type=F32)
        acc[...] += jnp.dot(pt_ref[0, :, here], ng, preferred_element_type=F32)
        return 0

    lax.fori_loop(0, tiles_of(count), step, 0)
    for o in range(shards):
        gn_ref[o] = acc[:, o * npp : (o + 1) * npp].astype(BF16)


def span_grads(live, negatives, p, pt, grad_products, first, count):
    shards, width, lanes = negatives.shape
    npp = lanes // count
    spans, length, _ = p.shape
    later = grad_products is not None
    return pl.pallas_call(
        functools.partial(later_span_kernel if later else span_kernel, first=first),
        grid_spec=pltpu.PrefetchScalarGridSpec(
            num_scalar_prefetch=1,
            grid=(count,),
            in_specs=[
                pl.BlockSpec((shards, width, npp), lambda s, *_: (0, 0, s)),
                pl.BlockSpec((1, length, 512), lambda s, *_: (s + first, 0, 0)),
                pl.BlockSpec((1, width, length), lambda s, *_: (s + first, 0, 0)),
            ]
            + ([pl.BlockSpec(memory_space=pl.ANY)] if later else []),
            out_specs=[
                pl.BlockSpec((1, length, 512), lambda s, *_: (s + first, 0, 0)),
                pl.BlockSpec((shards, width, npp), lambda s, *_: (0, 0, s)),
            ],
            scratch_shapes=[
                pltpu.VMEM((512, shards * npp), BF16),
                pltpu.VMEM((width, shards * npp), F32),
            ],
        ),
        out_shape=[
            jax.ShapeDtypeStruct((spans, length, 512), F32),
            jax.ShapeDtypeStruct((shards, width, lanes), BF16),
        ],
        input_output_aliases={4: 0} if later else {},
        compiler_params=params(),
        cost_estimate=cost(count * 6 * length * 512 * shards * npp, 8 * count * length * 512),
        name="span_grads",
    )(live, negatives, p, pt, *([grad_products] if later else []))


def source_kernel(
    src_idx, rel_idx, live, gp_ref, src_ref, rel_ref, tgt_ref, gl_in, gk_in, gl4, gk4, st_s, st_r, *, first
):
    span = pl.program_id(0)

    @pl.when(span == 0)
    def _():
        if gl_in is None:
            gl4[...] = jnp.zeros(gl4.shape, F32)
            gk4[...] = jnp.zeros(gk4.shape, F32)
        else:
            gl4[...] = gl_in[...]
            gk4[...] = gk_in[...]

    def one_tile(tile, _):
        base = pl.multiple_of(tile * TILE, TILE)
        sub = 32
        lane = lax.broadcasted_iota(jnp.int32, (sub, LANES), 1)
        low = lane < 72

        @pl.loop(0, TILE, step=sub)
        def _(r0):
            r0 = pl.multiple_of(r0, sub)
            here = pl.ds(pl.multiple_of(base + r0, sub), sub)
            n, s, r, t = (
                [ref[0, here, j * LANES : (j + 1) * LANES] for j in range(4)]
                for ref in (gp_ref, src_ref, rel_ref, tgt_ref)
            )
            re0 = n[0] + t[0]
            re1 = n[1] + t[1]
            im0 = pltpu.roll(jnp.where(low, n[2], n[1]), 56, 1) + t[2]
            im1 = pltpu.roll(jnp.where(low, n[3], n[2]), 56, 1) + t[3]
            for other, stage in ((r, st_s), (s, st_r)):
                grads = (
                    re0 * other[0] + im0 * other[2],
                    re1 * other[1] + im1 * other[3],
                    im0 * other[0] - re0 * other[2],
                    im1 * other[1] - re1 * other[3],
                )
                for j in range(4):
                    stage[column(r0, j, sub), :] = grads[j]

        @pl.loop(0, TILE, step=GROUP)
        def _(r0):
            for v in range(0, GROUP, 2):
                add_rows(((src_idx, gl4, st_s), (rel_idx, gk4, st_r)), first + span, base + r0 + v, r0, v, 2)

        return 0

    lax.fori_loop(0, tiles_of(live[first + span]), one_tile, 0)


def first_source_kernel(src_idx, rel_idx, live, gp, src, rel, tgt, gl4, gk4, st_s, st_r, *, first):
    source_kernel(src_idx, rel_idx, live, gp, src, rel, tgt, None, None, gl4, gk4, st_s, st_r, first=first)


def source_grads(src_idx, rel_idx, live, gp, src, rel, tgt, totals, sizes, first, count):
    spans, length = src_idx.shape
    row_spec = pl.BlockSpec((1, length, 512), lambda s, *_: (s + first, 0, 0))
    outs = [whole((n, LANES)) for n in sizes]
    body = first_source_kernel if totals is None else source_kernel
    return pl.pallas_call(
        functools.partial(body, first=first),
        grid_spec=pltpu.PrefetchScalarGridSpec(
            num_scalar_prefetch=3,
            grid=(count,),
            in_specs=[row_spec] * 4 + ([] if totals is None else outs),
            out_specs=outs,
            scratch_shapes=[pltpu.VMEM((PITCH * TILE, LANES), F32)] * 2,
        ),
        out_shape=[jax.ShapeDtypeStruct((n, LANES), F32) for n in sizes],
        compiler_params=params(),
        cost_estimate=cost(0, 30e6 * count),
        name="source_grads",
    )(src_idx, rel_idx, live, gp, src, rel, tgt, *(totals or ()))


def joined(ref, b, width):
    return [
        ref[pl.ds(4 * LANES * b + j, LANES, stride=4), :].T[:size]
        for j, (_, size) in enumerate(parts_of(width))
    ]


def relation_kernel(g_ref, t_ref, s_ref, _, o_ref, *, width, rows, spare):
    grads = [g_ref[pl.ds(j, rows, stride=4), :] for j in range(4)]
    square = grads[0] * grads[0] + grads[1] * grads[1] + grads[2] * grads[2] + grads[3] * grads[3]
    state = s_ref[...] + jnp.sum(square, -1, keepdims=True) * (1.0 / width)
    scale = LEARN_RATE / (jnp.sqrt(state) + EPSILON)
    lane = lax.broadcasted_iota(jnp.int32, (rows, LANES), 1)
    for j in range(4):
        new = t_ref[pl.ds(j, rows, stride=4), :] - grads[j] * scale
        if j == 1:
            new = jnp.where(lane == spare, state, new)
        o_ref[pl.ds(j, rows, stride=4), :] = new


def update_relations(g4, t4, state, held, width):
    rows = state.shape[0]
    spare = parts_of(width)[1][1]
    full = [pl.BlockSpec(x.shape, lambda: (0, 0)) for x in (g4, t4, state)]
    return pl.pallas_call(
        functools.partial(relation_kernel, width=width, rows=rows, spare=spare),
        in_specs=full + [pl.BlockSpec(memory_space=pl.ANY)],
        out_specs=full[0],
        out_shape=jax.ShapeDtypeStruct(g4.shape, F32),
        compiler_params=params(),
        cost_estimate=cost(0, 3e6),
        name="update_relations",
    )(g4, t4, state, held)


def join_kernel(g_ref, o_ref, s_ref, *, width, cols):
    spare = parts_of(width)[1][1]
    for b in range(cols // LANES):
        here = slice(b * LANES, min((b + 1) * LANES, o_ref.shape[1]))
        count = here.stop - here.start
        for j, (start, size) in enumerate(parts_of(width)):
            x = g_ref[pl.ds(4 * LANES * b + j, LANES, stride=4), :].T
            o_ref[start : start + size, here] = x[:size, :count]
            if j == 1:
                s_ref[:, here] = x[spare : spare + 1, :count]


def join_relations(rows4, width, kinds):
    return pl.pallas_call(
        functools.partial(join_kernel, width=width, cols=rows4.shape[0] // 4),
        in_specs=[pl.BlockSpec(rows4.shape, lambda: (0, 0))],
        out_specs=[pl.BlockSpec((width, kinds), lambda: (0, 0)), pl.BlockSpec((1, kinds), lambda: (0, 0))],
        out_shape=[jax.ShapeDtypeStruct((width, kinds), F32), jax.ShapeDtypeStruct((1, kinds), F32)],
        compiler_params=params(),
        cost_estimate=cost(0, 4 * kinds * (width + 512)),
        name="join_relations",
    )(rows4)


def update(grad, t_ref, s_ref, q_ref, m_ref, start, size):
    here = slice(start, start + size)
    width = t_ref.shape[0]
    state = s_ref[0:1, here] + jnp.sum(grad * grad, 0, keepdims=True) * (1.0 / width)
    new = t_ref[:, here] - grad * (LEARN_RATE / (jnp.sqrt(state) + EPSILON))
    top = jnp.max(jnp.abs(new), 0, keepdims=True)
    code = new * (CODE / jnp.maximum(top, 1e-30))
    q_ref[:, here] = jnp.round(code).astype(jnp.int32).astype(jnp.int16)
    m_ref[0:1, here] = top
    m_ref[1:2, here] = state


def left_kernel(g_ref, t_ref, s_ref, q_ref, m_ref, *, width, cols):
    for b in range(cols // LANES):
        grad = jnp.concatenate(joined(g_ref, b, width), 0)
        update(grad, t_ref, s_ref, q_ref, m_ref, b * LANES, LANES)


def coded_shapes(width, rows):
    return [jax.ShapeDtypeStruct((width, rows), jnp.int16), jax.ShapeDtypeStruct((2, rows), F32)]


def update_left(g4, table_t, state, cols, start, blocks):
    width, rows = table_t.shape
    return pl.pallas_call(
        functools.partial(left_kernel, width=width, cols=cols),
        grid=(blocks,),
        in_specs=[
            pl.BlockSpec((4 * cols, LANES), lambda i: (i + start, 0)),
            pl.BlockSpec((width, cols), lambda i: (0, i + start)),
            pl.BlockSpec((1, cols), lambda i: (0, i + start)),
        ],
        out_specs=[pl.BlockSpec((width, cols), lambda i: (0, i)), pl.BlockSpec((2, cols), lambda i: (0, i))],
        out_shape=coded_shapes(width, blocks * cols),
        compiler_params=params(),
        cost_estimate=cost(0, 10 * blocks * cols * width),
        name="update_left",
    )(g4, table_t, state)


def negative_sum(acc, idx_ref, b_ref, cols, step, start=0):
    shards, _, lanes = b_ref.shape
    row = lax.broadcasted_iota(jnp.int16, (cols, step), 0)
    one, zero = jnp.ones((), BF16), jnp.zeros((), BF16)
    for q in range(shards):
        for k in range(0, lanes, step):
            idx = (idx_ref[q, :, k : k + step] - (pl.program_id(0) + start) * cols).astype(jnp.int16)
            hot = jnp.where(row == idx, one, zero)
            acc += lax.dot_general(
                b_ref[q, :, k : k + step], hot, (((1,), (1,)), ((), ())), preferred_element_type=F32
            )
    return acc


def first_spread_kernel(idx_ref, b_ref, o_ref, *, cols, step):
    o_ref[...] = negative_sum(jnp.zeros(o_ref.shape, F32), idx_ref, b_ref, cols, step)


def spread_kernel(g_ref, g4_ref, idx_ref, b_ref, o_ref, *, cols, step):
    o_ref[...] = negative_sum(g_ref[...], idx_ref, b_ref, cols, step)
    width = o_ref.shape[0]
    for b in range(cols // LANES):
        for (start, size), x in zip(parts_of(width), joined(g4_ref, b, width)):
            o_ref[start : start + size, b * LANES : (b + 1) * LANES] += x


def spread_update_kernel(g_ref, idx_ref, b_ref, t_ref, s_ref, q_ref, m_ref, acc, *, cols, step, start):
    acc[...] = negative_sum(g_ref[...], idx_ref, b_ref, cols, step, start)
    for b in range(cols // LANES):
        update(acc[:, b * LANES : (b + 1) * LANES], t_ref, s_ref, q_ref, m_ref, b * LANES, LANES)


def spread(grads, idx, returned, rows, cols):
    shards, width, lanes = returned.shape
    block = pl.BlockSpec((width, cols), lambda i: (0, i))
    return pl.pallas_call(
        functools.partial(
            spread_kernel if grads else first_spread_kernel,
            cols=cols, step=2 * LANES if lanes % 256 == 0 else LANES,
        ),
        grid=(rows // cols,),
        in_specs=([block, pl.BlockSpec((4 * cols, LANES), lambda i: (i, 0))] if grads else [])
        + [whole(idx.shape), whole(returned.shape)],
        out_specs=block,
        out_shape=jax.ShapeDtypeStruct((width, rows), F32),
        compiler_params=params(),
        cost_estimate=cost(2 * width * rows * shards * lanes, 8 * width * rows),
        name="spread",
    )(*grads, idx, returned)


def spread_update(grad_t, idx, returned, table_t, state, cols, start, blocks):
    width, rows = grad_t.shape
    shards, _, lanes = returned.shape
    here = pl.BlockSpec((width, cols), lambda i: (0, i + start))
    return pl.pallas_call(
        functools.partial(
            spread_update_kernel, cols=cols, step=2 * LANES if lanes % 256 == 0 else LANES, start=start
        ),
        grid=(blocks,),
        in_specs=[
            here, whole(idx.shape), whole(returned.shape), here, pl.BlockSpec((1, cols), lambda i: (0, i + start)),
        ],
        out_specs=[pl.BlockSpec((width, cols), lambda i: (0, i)), pl.BlockSpec((2, cols), lambda i: (0, i))],
        out_shape=coded_shapes(width, blocks * cols),
        scratch_shapes=[pltpu.VMEM((width, cols), F32)],
        compiler_params=params(),
        cost_estimate=cost(2 * width * blocks * cols * shards * lanes, 8 * width * blocks * cols),
        name="spread_update",
    )(grad_t, idx, returned, table_t, state)


def decode_kernel(m_ref, *refs, ways):
    code = sum(ref[...].astype(jnp.int32) for ref in refs[:ways])
    refs[-1][...] = code.astype(F32) * (m_ref[0:1, :] * (1.0 / CODE))


def decode(codes, meta, rows, cols, start, table_t):
    width, count = codes[0].shape
    ways = len(codes)
    block = pl.BlockSpec((width, cols), lambda i: (0, i))
    return pl.pallas_call(
        functools.partial(decode_kernel, ways=ways),
        grid=(count // cols,),
        in_specs=[pl.BlockSpec((2, cols), lambda i: (0, i + start))]
        + [block] * ways
        + ([] if table_t is None else [pl.BlockSpec(memory_space=pl.ANY)]),
        out_specs=pl.BlockSpec((width, cols), lambda i: (0, i + start)),
        out_shape=jax.ShapeDtypeStruct((width, rows), F32),
        input_output_aliases={} if table_t is None else {1 + ways: 0},
        compiler_params=params(),
        cost_estimate=cost(0, 6 * width * count),
        name="decode",
    )(meta, *codes, *([] if table_t is None else [table_t]))


def passed_along(block, axis, distance):
    devices = range(lax.axis_size(axis))
    route = [((i - distance) % len(devices), i) for i in devices]
    return lax.ppermute(block, axis, route)


def corner_senders(n):
    return [i for i in range(n) if i % 4 == 1]


def handed_over(halves, held, before_meta=()):
    (first, meta_a), (second, meta_b) = halves
    n = lax.axis_size("grp")
    turning = corner_senders(n)
    there = lax.ppermute(first, "grp", [(i, (i + ROUND - 1) % n) for i in turning])
    straight = lax.ppermute(first, "grp", [(i, (i + ROUND) % n) for i in range(n) if i not in turning])
    other = passed_along(second, "grp", ROUND)
    meta = after(jnp.concatenate([meta_a, meta_b], 1), *before_meta)
    meta = passed_along(meta, "grp", ROUND)
    here = lax.ppermute(
        after(there, *held), "grp", [((i + ROUND - 1) % n, (i + ROUND) % n) for i in turning]
    )
    return ((straight, here), (other,)), meta, there


def decoded(arrived, rows, cols, held):
    table, start = None, 0
    halves, meta = arrived[:2]
    for codes in halves:
        table = decode((after(codes[0], *held), *codes[1:]), meta, rows, cols, start, table)
        start += codes[0].shape[1] // cols
    return table, meta[1]


def exchanged(blocks):
    return lax.all_to_all(blocks, "shard", split_axis=0, concat_axis=0, tiled=True)


def after(value, *others):
    return lax.optimization_barrier((value, *others))[0]


def local(
    left_table,
    right_table,
    left_state,
    right_state,
    relations,
    relation_state,
    source_rows,
    relation_ids,
    target_rows,
    negative_rows,
    span_sizes,
):
    shards = lax.axis_size("shard")
    spans, span_len = source_rows.shape
    neg_per = negative_rows.shape[1] // shards
    npp = round_up(neg_per, LANES)
    rows, width = left_table.shape
    kinds = relations.shape[0]
    kinds_up = round_up(kinds, LANES)
    length = round_up(span_len, TILE)

    left_t, right_t, rel_t = left_table.T, right_table.T, relations.T
    live = span_sizes[0]

    ids = negative_rows.reshape(spans, shards, neg_per)
    ids = jnp.pad(ids, ((0, 0), (0, 0), (0, npp - neg_per)), constant_values=-1)
    asked = lax.all_to_all(ids.transpose(1, 0, 2), "shard", split_axis=0, concat_axis=0, tiled=True)
    asked_lanes = asked.reshape(shards, spans, 1, npp)

    src_idx, rel_idx, tgt_idx = (
        jnp.pad(a, ((0, 0), (0, length - span_len))) for a in (source_rows, relation_ids, target_rows)
    )

    third = -(-spans // 3)
    (c0, c1, c2) = [(a, min(third, spans - a)) for a in range(0, spans, third)]

    served0 = serve(asked_lanes, right_t, *c0)
    fetched0 = exchanged(served0)
    served1 = serve(after(asked_lanes, served0), right_t, *c1)
    served2 = serve(after(asked_lanes, served1), right_t, *c2)
    left4 = split_rows(after(left_t, served2), 512)
    right4 = split_rows(after(right_t, served2), 512)
    rel4 = split_rows(after(rel_t, served2), kinds_up)

    fetched1 = exchanged(after(served1, left4, right4, rel4))
    p, pt, src, rel, tgt, gt = edges(
        src_idx, rel_idx, tgt_idx, live, after(left4, fetched0), rel4, right4, width
    )

    fetched2 = exchanged(after(served2, p))
    gp, gn0 = span_grads(live, after(fetched0, fetched1), p, pt, None, *c0)
    gp, gn1 = span_grads(live, fetched1, p, pt, gp, *c1)
    sizes = (4 * rows, 4 * kinds_up)
    sums = functools.partial(source_grads, src_idx, rel_idx, live)
    totals = sums(gp, src, rel, tgt, None, sizes, *c0)

    returned0 = exchanged(after(gn0, totals[1], fetched2))
    gp, gn2 = span_grads(live, fetched2, p, pt, after(gp, totals[1]), *c2)
    gl4, gk4 = sums(gp, src, rel, tgt, totals, sizes, c1[0], c1[1] + c2[1])

    returned1 = exchanged(after(gn1, gk4, returned0))
    rel_total4 = lax.psum_scatter(gk4, "grp", scatter_dimension=0, tiled=True)
    lanes0, lanes1, lanes2 = (
        asked[:, a : a + n].reshape(shards, 1, n * npp) for a, n in (c0, c1, c2)
    )
    blocks = rows // 512
    halves = ((0, blocks // 2), (blocks // 2, blocks - blocks // 2))
    left_in = after(left_t, gk4)
    coded_left = [tuple(update_left(gl4, left_in, left_state[None], 512, *half)) for half in halves]
    left_sent = tuple(c[1] for c in coded_left)
    gr4 = target_grads(tgt_idx, live, after(gt, *left_sent), 4 * rows)
    moved_left = handed_over(coded_left, (gr4,))

    returned2 = exchanged(after(gn2, gr4, moved_left[2], moved_left[0][0][0], returned1))
    rel_sum4 = lax.psum(after(rel_total4, gr4), "shard")
    grad_right = spread((), lanes0, after(returned0, gr4), rows, 512)
    grad_right = spread((grad_right, gr4), lanes1, returned1, rows, 512)
    grad_right = after(grad_right, *moved_left[0][0], *moved_left[0][1], moved_left[1])

    coded = []
    for half in halves:
        coded.append(
            tuple(spread_update(grad_right, lanes2, returned2, right_t, right_state[None], 512, *half))
        )
        grad_right = after(grad_right, coded[-1][1])
    new_left, new_left_state = decoded(moved_left, rows, 512, (coded[1][1],))
    slice_rows = kinds_up // lax.axis_size("grp")
    place = lax.axis_index("grp") * slice_rows
    own_rel4 = lax.dynamic_slice(rel4, (4 * place, 0), (4 * slice_rows, LANES))
    own_state = lax.dynamic_slice(
        jnp.pad(relation_state, (0, kinds_up - kinds))[:, None], (place, 0), (slice_rows, 1)
    )
    new_rel4 = update_relations(rel_sum4, own_rel4, own_state, coded[1][1], width)
    new_rel4 = lax.all_gather(new_rel4, "grp", axis=0, tiled=True)
    new_rel_t, new_relation_state = join_relations(new_rel4, width, kinds)
    moved_right = handed_over(coded, (coded[1][1],), (new_rel_t,))
    new_right, new_right_state = decoded(moved_right, rows, 512, (new_left, new_rel_t))
    return (new_left.T, new_left_state, new_right.T, new_right_state, new_rel_t.T, new_relation_state[0])


def solution(mesh):
    rows2, rows1 = P(("grp", "shard"), None), P(("grp", "shard"))
    return jax.shard_map(
        local,
        mesh=mesh,
        in_specs=(rows2, rows2, rows1, rows1, P(), P(), rows2, rows2, rows2, rows2, rows2),
        out_specs=(rows2, rows1, rows2, rows1, P(), P()),
        check_vma=False,
    )
```
